768 devices in a mesh: blk: 16 (over z_hi, x), grp: 48 (over y, z_lo, core).
Axes of the slice: x: 4, y: 8, z: 12 (z_hi: 4, z_lo: 3; z = z_hi * 3 + z_lo), core: 2. Of those that a mesh axis runs over, the one named last changes fastest.
Arguments:
- query_states: bfloat16 [16, 48, 128, 1024], P('blk', 'grp'), may hold values from -96 to 96
- passages: bfloat16 [16, 48, 128, 1024], P('blk', 'grp'), may hold values from -6 to 6
- proj_weight: bfloat16 [1024, 1024], replicated, may hold values from -0.2 to 1.2
- neg_store: bfloat16 [16, 48, 512, 1024], P('blk', 'grp'), may hold values from -12 to 12
- positive: int32 [16, 48, 128], P('blk', 'grp'), may hold values from 0 to 127, each once within a row
- neg_owner: int32 [16, 48, 896, 1], P('blk', 'grp'), may hold values from 0 to 15; in each aligned block of 896 rows (0 to 895, 896 to 1791, ..., all dimensions but the last counted through in order) at most 64 rows name the same one
- neg_slot: int32 [16, 48, 128, 7], P('blk', 'grp'), may hold values from 0 to 511
- neg_count: int32 [16, 48, 128], P('blk', 'grp'), may hold values from 1 to 7
Outputs:
- state_grads: bfloat16 [16, 48, 128, 1024], P('blk', 'grp')
- passage_grads: bfloat16 [16, 48, 128, 1024], P('blk', 'grp')
- weight_grad: float32 [1024, 1024], P('blk')
The draws below stay inside these ranges and needn't reach their ends.
Inputs may be any that keep to these rules, and one draw needn't show every extreme that they name: `neg_owner`: among the 896 slots of one device no owner is named more than 64 times, a bound that some block reaches.
All inputs are finite; a program needn't handle non-finite values.
Results may differ from the reference program's by a relative error of at most 0.017.
Values may be sent and summed in bfloat16 or wider, within the bound.
No kernel may reach another device: no remote copies, remote signals or barrier semaphores. Data moves between devices by JAX's collectives and lax.ppermute only.
A program may use at most 64 MiB of HBM per device.

```python
import math
import jax
import jax.numpy as jnp
import numpy as np
from jax import lax

D = 1024
ROWS = 128
POOL = 512
NEG = 7
STOPS = 4
CAP = 64
N_BLK = 16
N_GRP = 48


def shared_base(key):
    return jnp.clip(jax.random.normal(key, (N_BLK, N_GRP, ROWS, D), jnp.float32), -6.0, 6.0)


def draw_passages(key, part):
    base = shared_base(key)
    return base.astype(jnp.bfloat16)


def draw_query_states(key, part):
    key = jax.random.fold_in(key, 5)
    return jnp.clip(jax.random.normal(key, (N_BLK, N_GRP, ROWS, D), jnp.float32), -6.0, 6.0).astype(jnp.bfloat16)


def draw_proj_weight(key, part):
    key = jax.random.fold_in(key, 9)
    noise = jnp.clip(jax.random.normal(key, (D, D), jnp.float32), -3.0, 3.0) * (0.5 / D ** 0.5)
    rowid = lax.broadcasted_iota(jnp.int32, (D, D), 0)
    colid = lax.broadcasted_iota(jnp.int32, (D, D), 1)
    return (jnp.where(rowid == colid, 1.0, 0.0) + noise).astype(jnp.bfloat16)


def with_ends(array, stream_key, smallest, largest):
    longest = array.shape.index(max(array.shape))
    spots = []
    for shift in (0, 1):
        where = [jax.random.randint(jax.random.fold_in(stream_key, axis), (), 0, length) for axis, length in enumerate(array.shape)]
        where[longest] = (where[longest] + shift) % array.shape[longest]
        spots.append(tuple(where))
    return array.at[spots[0]].set(smallest).at[spots[1]].set(largest)


def block_levels(key, extent, pieces, smallest, top_value):
    gain = 1.0
    for axis_at, blocks in pieces:
        steps = jax.random.uniform(jax.random.fold_in(jax.random.fold_in(key, 6), axis_at), (blocks,), jnp.float32, smallest / len(pieces), top_value / len(pieces))
        gain = gain * jnp.repeat(jnp.exp(steps), extent[axis_at] // blocks).reshape((-1,) + (1,) * (len(extent) - 1 - axis_at))
    return gain


def deal_out(key, own, number, rows, number_of, top, bound, skew):
    order = jax.random.permutation(key, number_of)
    packed, usual = shares(number_of, rows * top, bound, skew, True), shares(number_of, rows * top, bound, skew, False)
    places = jnp.arange(number_of)

    def named(lengths, offset_by):
        used = int((lengths > 0).sum())
        fixed = max(1, used // 4)
        moved = fixed + (places - fixed + offset_by * (used - fixed)) % max(1, number_of - fixed)
        return jnp.zeros((number_of,), jnp.int32).at[order[jnp.where(places < fixed, places, moved)]].set(jnp.asarray(lengths, jnp.int32))

    lengths = jnp.where(number % 4 == 0, named(packed, number // 4), named(usual, number - number // 4 - 1))
    mixed = jax.random.permutation(jax.random.fold_in(own, 3), number_of)
    giver, taker = mixed[0:number_of // 2 * 2:2], mixed[1:number_of // 2 * 2:2]
    margin = jnp.minimum(lengths[giver] - 1, bound - lengths[taker]) // 2
    margin = jnp.where((giver == order[0]) | (taker == order[0]) | (lengths[taker] == 0), 0, jnp.maximum(margin, 0))
    moved = jax.random.randint(jax.random.fold_in(own, 4), (number_of // 2,), 0, 1 << 20) % (margin + 1)
    lengths = lengths.at[giver].add(-moved).at[taker].add(moved)
    items = jnp.searchsorted(jnp.cumsum(lengths), jnp.arange(rows * top), side="right").astype(jnp.int32)
    listing = items.reshape(top, rows).T
    listing = listing[jax.random.permutation(jax.random.fold_in(own, 1), rows)]
    offset_by = jax.random.randint(jax.random.fold_in(own, 2), (rows, 1), 0, top)
    return jnp.take_along_axis(listing, (jnp.arange(top)[None, :] + offset_by) % top, axis=1)


def shares(count, total, reach, lean, full):
    loads = [(1 << 20) // math.isqrt(grade ** lean) + 1 for grade in range(1, count + 1)]
    largest = reach if full else min(reach, max(-(-total // count), total * loads[0] // sum(loads)))
    least = 1 if total - largest >= count - 1 else 0
    counts, spare = [largest] + [least] * (count - 1), total - largest - least * (count - 1)
    while spare > 0:
        candidates = [i for i in range(1, count) if counts[i] < largest] or [i for i in range(1, count) if counts[i] < reach]
        pool, remaining = sum([loads[i] for i in candidates]), spare
        for i in candidates:
            extra = min(reach - counts[i], max(1, remaining * loads[i] // pool), spare)
            counts[i] = counts[i] + extra
            spare = spare - extra
    return np.array(counts)


def centred(own_key, dims, scale, reach, shards=(), kind=jnp.bfloat16):
    array = scale * jax.random.normal(own_key, dims, jnp.float32)
    if shards:
        array = array * block_levels(own_key, dims, shards, -0.22, 0.18)
    return jnp.clip(array, -reach, reach).astype(kind)


def setup_inputs(seed: int = 0) -> dict:
    arg_keys = jax.random.split(jax.random.key(seed), 9)
    query_states = draw_query_states(jax.random.fold_in(arg_keys[8], 71), 0)
    passages = draw_passages(jax.random.fold_in(arg_keys[8], 71), 0)
    proj_weight = draw_proj_weight(jax.random.fold_in(arg_keys[8], 71), 0)
    neg_store = centred(arg_keys[3], (N_BLK, N_GRP, POOL, D), 2.0, 12.0, ((0, 16), (1, 48)))
    positive = jax.vmap(lambda own: jax.random.permutation(own, ROWS))(jax.random.split(arg_keys[4], N_BLK * N_GRP)).reshape((N_BLK, N_GRP, ROWS)).astype(jnp.int32)
    neg_owner_keys = jax.random.split(jax.random.fold_in(arg_keys[5], 1), N_BLK * N_GRP * (ROWS * NEG) // (ROWS * NEG))
    neg_owner_turns = jax.random.permutation(jax.random.fold_in(arg_keys[5], 3), N_BLK * N_GRP * (ROWS * NEG) // (ROWS * NEG))
    neg_owner = jax.vmap(lambda own, number: deal_out(jax.random.fold_in(arg_keys[5], 2), own, number, ROWS * NEG, N_BLK, 1, CAP, 2))(neg_owner_keys, neg_owner_turns).reshape((N_BLK, N_GRP, ROWS * NEG, 1))
    neg_slot = with_ends(jax.random.randint(arg_keys[6], (N_BLK, N_GRP, ROWS, NEG), 0, POOL), jax.random.fold_in(arg_keys[6], 1), 0, POOL - 1).astype(jnp.int32)
    neg_count = with_ends(jax.random.randint(arg_keys[7], (N_BLK, N_GRP, ROWS), 1, NEG + 1), jax.random.fold_in(arg_keys[7], 1), 1, NEG).astype(jnp.int32)
    return {"query_states": query_states, "passages": passages, "proj_weight": proj_weight, "neg_store": neg_store, "positive": positive, "neg_owner": neg_owner, "neg_slot": neg_slot, "neg_count": neg_count}


def reference(query_states, passages, proj_weight, neg_store, positive, neg_owner, neg_slot, neg_count):
    factor = D ** -0.5
    flat_states = query_states.reshape(-1, D)
    queries = jnp.dot(flat_states, proj_weight, preferred_element_type=jnp.float32).astype(jnp.bfloat16)
    queries = queries.reshape(N_BLK, N_GRP, ROWS, D)
    owners = neg_owner.reshape(N_BLK, N_GRP, ROWS, NEG)
    group_ids = jnp.arange(N_GRP, dtype=jnp.int32)[:, None, None]

    def one_column(carry, index):
        shifted = ((index - jnp.arange(STOPS, dtype=jnp.int32)) % N_BLK).astype(jnp.int32)
        blocks = jnp.take(passages, shifted, axis=0).astype(jnp.float32)
        negatives = neg_store[owners[index], group_ids, neg_slot[index]].astype(jnp.float32)
        mine = queries[index].astype(jnp.float32)
        batch = jnp.einsum("grd,sgkd->grsk", mine, blocks).reshape(N_GRP, ROWS, STOPS * ROWS) * factor
        negs = jnp.einsum("grd,grkd->grk", mine, negatives) * factor
        live = jnp.arange(NEG, dtype=jnp.int32)[None, None, :] < neg_count[index][:, :, None]
        negs = jnp.where(live, negs, -jnp.inf)
        top = jnp.maximum(jnp.max(batch, axis=2, keepdims=True), jnp.max(negs, axis=2, keepdims=True))
        batch_exp = jnp.exp(batch - top)
        neg_exp = jnp.exp(negs - top)
        total = jnp.sum(batch_exp, axis=2, keepdims=True) + jnp.sum(neg_exp, axis=2, keepdims=True)
        hit = (jnp.arange(STOPS * ROWS, dtype=jnp.int32)[None, None, :] == positive[index][:, :, None]).astype(jnp.float32)
        batch_grad = (batch_exp / total - hit).astype(jnp.bfloat16).astype(jnp.float32)
        neg_grad = (neg_exp / total).astype(jnp.bfloat16).astype(jnp.float32)
        batch_grad = batch_grad.reshape(N_GRP, ROWS, STOPS, ROWS)
        inner = jnp.einsum("grsk,sgkd->grd", batch_grad, blocks) + jnp.einsum("grk,grkd->grd", neg_grad, negatives)
        query_grad = (factor * inner).astype(jnp.bfloat16)
        parts = factor * jnp.einsum("grsk,grd->sgkd", batch_grad, mine)
        for stop in range(STOPS):
            carry = carry.at[shifted[stop]].add(parts[stop])
        return carry, query_grad

    start = jnp.zeros((N_BLK, N_GRP, ROWS, D), jnp.float32)
    summed, query_grads = lax.scan(one_column, start, jnp.arange(N_BLK, dtype=jnp.int32))
    passage_grads = summed.astype(jnp.bfloat16)
    flat_grads = query_grads.reshape(-1, D)
    state_grads = jnp.dot(flat_grads, proj_weight.T, preferred_element_type=jnp.float32).astype(jnp.bfloat16)
    weight_grad = jnp.dot(flat_states.T, flat_grads, preferred_element_type=jnp.float32)
    return state_grads.reshape(N_BLK, N_GRP, ROWS, D), passage_grads, weight_grad
```

```python
import jax
import jax.numpy as jnp
from jax import lax
from jax.experimental import pallas as pl
from jax.experimental.pallas import tpu as pltpu
from jax.sharding import Mesh, PartitionSpec as P

STOPS = 4
NEG = 7
CAP = 64
ROWS = 128
D = 1024
Z_HI, X, Y, Z_LO, CORE = 4, 4, 8, 3, 2
MEMBERS = Z_HI * X
SLOTS = MEMBERS * CAP
BLK = ("zh", "x")
GRP = ("y", "zl", "c")
F32 = jnp.float32
BF16 = jnp.bfloat16
VMEM_LIMIT = 40 * 1024 * 1024


def call(kernel, out_shape, *, flops=0, moved=0):
    return pl.pallas_call(
        kernel,
        out_shape=out_shape,
        compiler_params=pltpu.CompilerParams(vmem_limit_bytes=VMEM_LIMIT),
        cost_estimate=pl.CostEstimate(flops=flops, bytes_accessed=moved, transcendentals=0),
    )


def dot(left, right, on):
    return lax.dot_general(left, right, ((on[:1], on[1:]), ((), ())), preferred_element_type=F32)


def plan_kernel(owner_ref, slot_ref, count_ref, request_ref, mask_ref):
    owner = owner_ref[...]
    lane = lax.broadcasted_iota(jnp.int32, (ROWS, 128), 1)
    lane_owner, lane_j = lane % MEMBERS, lane // MEMBERS
    spread = jnp.full((ROWS, 128), -1, jnp.int32)
    for j in range(NEG):
        spread = jnp.where(lane_j == j, owner[:, j : j + 1], spread)
    named = (spread == lane_owner).astype(F32)
    row = lax.broadcasted_iota(jnp.int32, (ROWS, ROWS), 0)
    earlier = (lax.broadcasted_iota(jnp.int32, (ROWS, ROWS), 1) < row).astype(BF16)
    before = dot(earlier, named.astype(BF16), (1, 0))
    totals = jnp.broadcast_to(jnp.sum(named, axis=0, keepdims=True), (8, 128))
    src = lax.broadcasted_iota(jnp.int32, (128, 128), 0)
    dst = lax.broadcasted_iota(jnp.int32, (128, 128), 1)
    lower = (src % MEMBERS == dst % MEMBERS) & (src // MEMBERS < dst // MEMBERS)
    base = dot(totals.astype(BF16), lower.astype(F32).astype(BF16), (1, 0))[:1]
    place = named * (before + base + (lane_owner * CAP).astype(F32))
    slot = slot_ref[...]
    count = count_ref[...]
    column = lax.broadcasted_iota(jnp.int32, (ROWS, SLOTS), 1)
    wanted = jnp.zeros((ROWS, SLOTS), jnp.int32)
    used = jnp.zeros((ROWS, SLOTS), F32)
    for j in range(NEG):
        placed = jnp.sum(jnp.where(lane_j == j, place, 0.0), axis=1, keepdims=True).astype(jnp.int32)
        match = column == placed
        wanted = wanted + jnp.where(match, slot[:, j : j + 1], 0)
        live = (j < count).astype(F32)
        used = used + jnp.where(match, live, 0.0)
    mask_ref[...] = used.astype(BF16)
    request = jnp.sum(wanted, axis=0, keepdims=True)
    for owner_at in range(MEMBERS):
        request_ref[owner_at] = request[:, owner_at * CAP : (owner_at + 1) * CAP]


def serve_kernel(incoming_ref, store_ref, served_ref):
    pool = store_ref.shape[0]
    group = 4
    for at in range(0, MEMBERS, group):
        wanted = jnp.concatenate([incoming_ref[at + k] for k in range(group)], axis=1)
        row = lax.broadcasted_iota(jnp.int32, (pool, group * CAP), 0)
        pick = (row == wanted).astype(F32).astype(BF16)
        rows = dot(pick, store_ref[...], (0, 0)).astype(BF16)
        served_ref[at : at + group] = rows.reshape(group, CAP, D)


def attend_kernel(
    queries_ref, scores_ref, mask_ref, positive_ref, blocks_ref, replies_ref, batch_ref, query_ref
):
    factor = D**-0.5
    batch_scores = scores_ref[...]
    neg_scores = dot(queries_ref[...], replies_ref[...], (1, 1)) * factor
    neg_scores = jnp.where(mask_ref[...].astype(F32) > 0.5, neg_scores, -jnp.inf)
    top = jnp.maximum(
        jnp.max(batch_scores, axis=1, keepdims=True), jnp.max(neg_scores, axis=1, keepdims=True)
    )
    batch_exp = jnp.exp(batch_scores - top)
    neg_exp = jnp.exp(neg_scores - top)
    total = jnp.sum(batch_exp, axis=1, keepdims=True) + jnp.sum(neg_exp, axis=1, keepdims=True)
    column = lax.broadcasted_iota(jnp.int32, (ROWS, STOPS * ROWS), 1)
    hit = (column == positive_ref[...]).astype(F32)
    batch_grad = (batch_exp / total - hit).astype(BF16)
    neg_grad = (neg_exp / total).astype(BF16)
    batch_ref[...] = batch_grad
    inner = dot(batch_grad, blocks_ref[...], (1, 0)) + dot(neg_grad, replies_ref[...], (1, 0))
    query_ref[...] = (factor * inner).astype(BF16)


def around(x, axis, by):
    count = lax.axis_size(axis)
    return lax.ppermute(x, axis, [(i, (i + by) % count) for i in range(count)])


def swap(x, axis):
    return lax.all_to_all(x, axis, split_axis=0, concat_axis=0, tiled=True)


def local(query_states, passages, proj_weight, neg_store, positive, neg_owner, neg_slot, neg_count):
    factor = D**-0.5
    states = query_states.reshape(ROWS, D)
    own = passages.reshape(ROWS, D)
    store = neg_store.reshape(-1, D)
    x_at = lax.axis_index("x")

    request, mask = call(
        plan_kernel,
        (
            jax.ShapeDtypeStruct((MEMBERS, 1, CAP), jnp.int32),
            jax.ShapeDtypeStruct((ROWS, SLOTS), BF16),
        ),
        moved=1 << 20,
    )(neg_owner.reshape(ROWS, NEG), neg_slot.reshape(ROWS, NEG), neg_count.reshape(ROWS, 1))
    incoming = swap(request, BLK)
    served = call(
        serve_kernel,
        jax.ShapeDtypeStruct((MEMBERS, CAP, D), BF16),
        flops=2 * SLOTS * store.shape[0] * D,
        moved=3 << 20,
    )(incoming, store)
    replies = swap(served, BLK).reshape(SLOTS, D)

    queries = jnp.dot(states, proj_weight, preferred_element_type=F32).astype(BF16)
    below = around(own, "zh", 1)
    above = around(queries, "zh", -1)
    target = jnp.arange(X, dtype=jnp.int32)[:, None, None]
    to_row = jnp.concatenate(
        [
            jnp.where(target >= x_at, own[None], below[None]),
            jnp.where(target <= x_at, queries[None], above[None]),
        ],
        axis=1,
    )
    from_row = swap(to_row, "x")
    blocks = [own]
    asking = [queries]
    for stop in range(1, STOPS):
        blocks.append(lax.dynamic_index_in_dim(from_row, (x_at - stop) % X, 0, False)[:ROWS])
        asking.append(lax.dynamic_index_in_dim(from_row, (x_at + stop) % X, 0, False)[ROWS:])
    blocks = jnp.concatenate(blocks, axis=0)
    asking = jnp.concatenate(asking, axis=0)
    scores = dot(queries, blocks, (1, 1)) * factor

    quarter = states.reshape(ROWS, Z_HI, X, D // MEMBERS)
    quarter = quarter.transpose(2, 0, 1, 3).reshape(X, 1, ROWS, D // X)
    quarter = jnp.broadcast_to(quarter, (X, CORE, ROWS, D // X)).reshape(X * CORE, ROWS, D // X)
    row_states = swap(quarter, ("x", "c")).reshape(X * CORE * ROWS, D // X)

    batch_grad, query_grad = call(
        attend_kernel,
        (
            jax.ShapeDtypeStruct((ROWS, STOPS * ROWS), BF16),
            jax.ShapeDtypeStruct((ROWS, D), BF16),
        ),
        flops=2 * ROWS * D * (2 * SLOTS + STOPS * ROWS),
        moved=4 << 20,
    )(queries, scores, mask, positive.reshape(ROWS, 1), blocks, replies)

    half = query_grad.reshape(ROWS, CORE, D // CORE).transpose(1, 0, 2)[None]
    half = jnp.broadcast_to(half, (X, CORE, ROWS, D // CORE)).reshape(X * CORE, ROWS, D // CORE)
    row_grads = swap(half, ("x", "c")).reshape(X * CORE * ROWS, D // CORE)

    pieces = [batch_grad[:, :ROWS]]
    for stop in range(1, STOPS):
        piece = batch_grad[:, stop * ROWS : (stop + 1) * ROWS]
        pieces.append(
            lax.ppermute(
                piece, BLK, [(i, (i - stop) % MEMBERS) for i in range(MEMBERS)]
            )
        )
    passage_grads = factor * dot(jnp.concatenate(pieces, axis=0), asking, (0, 0))
    state_grads = dot(query_grad, proj_weight, (1, 1))

    part = dot(row_states, row_grads, (0, 0)).astype(BF16)
    part = swap(part.reshape(Z_HI * Y, D // MEMBERS // Y, D // CORE), ("zh", "y"))
    part = jnp.sum(part.astype(F32), axis=0).astype(BF16)
    parts = swap(jnp.broadcast_to(part[None], (Y * Z_LO * CORE,) + part.shape), GRP)
    parts = parts.reshape(Y, Z_LO, CORE, D // MEMBERS // Y, D // CORE)
    weight_grad = jnp.sum(parts.astype(F32), axis=1).transpose(0, 2, 1, 3)
    return (
        state_grads.astype(BF16).reshape(query_states.shape),
        passage_grads.astype(BF16).reshape(passages.shape),
        weight_grad.reshape(D // MEMBERS, D),
    )


def solution(mesh):
    fine = Mesh(mesh.devices.reshape(Z_HI, X, Y, Z_LO, CORE), ("zh", "x", "y", "zl", "c"))
    placed = (
        P(BLK, GRP, None, None),
        P(BLK, GRP, None, None),
        P(),
        P(BLK, GRP, None, None),
        P(BLK, GRP, None),
        P(BLK, GRP, None, None),
        P(BLK, GRP, None, None),
        P(BLK, GRP, None),
    )
    return jax.shard_map(
        local,
        mesh=fine,
        in_specs=placed,
        out_specs=(P(BLK, GRP, None, None), P(BLK, GRP, None, None), P(BLK, None)),
        check_vma=False,
    )
```

```python
import jax
import jax.numpy as jnp
from jax import lax
from jax.experimental import pallas as pl
from jax.experimental.pallas import tpu as pltpu
from jax.sharding import Mesh, PartitionSpec as P

STOPS = 4
NEG = 7
CAP = 64
ROWS = 128
D = 1024
Z_HI, X, Y, Z_LO, CORE = 4, 4, 8, 3, 2
MEMBERS = Z_HI * X
SLOTS = MEMBERS * CAP
BLK = ("zh", "x")
GRP = ("y", "zl", "c")
F32 = jnp.float32
BF16 = jnp.bfloat16
VMEM_LIMIT = 40 * 1024 * 1024


def call(kernel, out_shape, *, scalars=0, flops=0, moved=0):
    def run(*args):
        specs = [pl.BlockSpec(memory_space=pltpu.SMEM)] * scalars
        specs += [pl.BlockSpec(memory_space=pltpu.VMEM)] * (len(args) - scalars)
        return pl.pallas_call(
            kernel,
            out_shape=out_shape,
            in_specs=specs,
            compiler_params=pltpu.CompilerParams(vmem_limit_bytes=VMEM_LIMIT),
            cost_estimate=pl.CostEstimate(flops=flops, bytes_accessed=moved, transcendentals=0),
        )(*args)

    return run


def dot(left, right, on):
    return lax.dot_general(left, right, ((on[:1], on[1:]), ((), ())), preferred_element_type=F32)


def plan_kernel(owner_ref, slot_ref, count_ref, request_ref, mask_ref):
    owner = owner_ref[...]
    lane = lax.broadcasted_iota(jnp.int32, (ROWS, 128), 1)
    lane_owner, lane_j = lane % MEMBERS, lane // MEMBERS
    spread = jnp.full((ROWS, 128), -1, jnp.int32)
    for j in range(NEG):
        spread = jnp.where(lane_j == j, owner[:, j : j + 1], spread)
    named = (spread == lane_owner).astype(F32)
    row = lax.broadcasted_iota(jnp.int32, (ROWS, ROWS), 0)
    earlier = (lax.broadcasted_iota(jnp.int32, (ROWS, ROWS), 1) < row).astype(BF16)
    before = dot(earlier, named.astype(BF16), (1, 0))
    totals = jnp.broadcast_to(jnp.sum(named, axis=0, keepdims=True), (8, 128))
    src = lax.broadcasted_iota(jnp.int32, (128, 128), 0)
    dst = lax.broadcasted_iota(jnp.int32, (128, 128), 1)
    lower = (src % MEMBERS == dst % MEMBERS) & (src // MEMBERS < dst // MEMBERS)
    base = dot(totals.astype(BF16), lower.astype(F32).astype(BF16), (1, 0))[:1]
    place = named * (before + base + (lane_owner * CAP).astype(F32))
    slot = slot_ref[...]
    count = count_ref[...]
    column = lax.broadcasted_iota(jnp.int32, (ROWS, SLOTS), 1)
    wanted = jnp.zeros((ROWS, SLOTS), jnp.int32)
    used = jnp.zeros((ROWS, SLOTS), F32)
    for j in range(NEG):
        placed = jnp.sum(jnp.where(lane_j == j, place, 0.0), axis=1, keepdims=True).astype(jnp.int32)
        match = column == placed
        wanted = wanted + jnp.where(match, slot[:, j : j + 1], 0)
        live = (j < count).astype(F32)
        used = used + jnp.where(match, live, 0.0)
    mask_ref[...] = used.astype(BF16)
    request = jnp.sum(wanted, axis=0, keepdims=True)
    for owner_at in range(MEMBERS):
        request_ref[owner_at] = request[:, owner_at * CAP : (owner_at + 1) * CAP]


def serve_kernel(incoming_ref, store_ref, served_ref):
    pool = store_ref.shape[0]
    group = 4
    for at in range(0, MEMBERS, group):
        wanted = jnp.concatenate([incoming_ref[at + k] for k in range(group)], axis=1)
        row = lax.broadcasted_iota(jnp.int32, (pool, group * CAP), 0)
        pick = (row == wanted).astype(F32).astype(BF16)
        rows = dot(pick, store_ref[...], (0, 0)).astype(BF16)
        served_ref[at : at + group] = rows.reshape(group, CAP, D)


def attend_kernel(
    queries_ref,
    scores_ref,
    mask_ref,
    positive_ref,
    blocks_ref,
    replies_ref,
    batch_ref,
    query_ref,
    halves_ref,
):
    factor = D**-0.5
    batch_scores = scores_ref[...]
    neg_scores = dot(queries_ref[...], replies_ref[...], (1, 1)) * factor
    neg_scores = jnp.where(mask_ref[...].astype(F32) > 0.5, neg_scores, -jnp.inf)
    top = jnp.maximum(
        jnp.max(batch_scores, axis=1, keepdims=True), jnp.max(neg_scores, axis=1, keepdims=True)
    )
    batch_exp = jnp.exp(batch_scores - top)
    neg_exp = jnp.exp(neg_scores - top)
    total = jnp.sum(batch_exp, axis=1, keepdims=True) + jnp.sum(neg_exp, axis=1, keepdims=True)
    column = lax.broadcasted_iota(jnp.int32, (ROWS, STOPS * ROWS), 1)
    hit = (column == positive_ref[...]).astype(F32)
    batch_grad = (batch_exp / total - hit).astype(BF16)
    neg_grad = (neg_exp / total).astype(BF16)
    batch_ref[...] = batch_grad
    inner = dot(batch_grad, blocks_ref[...], (1, 0)) + dot(neg_grad, replies_ref[...], (1, 0))
    query_grad = (factor * inner).astype(BF16)
    query_ref[...] = query_grad
    for to in range(X * CORE):
        at = to % CORE * (D // CORE)
        halves_ref[to] = query_grad[:, at : at + D // CORE]


def pack_kernel(place_ref, own_ref, below_ref, queries_ref, above_ref, states_ref, pair_ref, *refs):
    x_at = place_ref[0]
    share = D // MEMBERS

    def columns(ref, x_to):
        piece = None
        for x_of in range(X):
            cut = [ref[:, (z * X + x_of) * share :][:, :share] for z in range(Z_HI)]
            cut = jnp.concatenate(cut, axis=1)
            piece = cut if piece is None else jnp.where(x_to == x_of, cut, piece)
        return piece

    *send_refs, mine_ref = refs
    mine_ref[0] = columns(states_ref, x_at)
    mine_ref[1] = columns(pair_ref, x_at)
    for step in range(1, X):
        send_ref = send_refs[step - 1]
        wraps = x_at + step >= X
        send_ref[:, :D] = jnp.where(wraps, below_ref[...], own_ref[...])
        send_ref[:, D : 2 * D] = jnp.where(wraps, queries_ref[...], above_ref[...])
        x_to = (x_at + step) % X
        send_ref[:, 2 * D : 2 * D + D // X] = columns(states_ref, x_to)
        send_ref[:, 2 * D + D // X :] = columns(pair_ref, x_to)


def scores_kernel(place_ref, own_ref, queries_ref, mine_ref, *refs):
    *got_refs, blocks_ref, asking_ref, states_ref, scores_ref = refs
    x_at, c_at = place_ref[0], place_ref[1]

    def place(x_from, c_from, value):
        at = pl.multiple_of((x_from * CORE + c_from) * ROWS, ROWS)
        states_ref[pl.ds(at, ROWS), :] = value

    blocks_ref[:ROWS] = own_ref[...]
    asking_ref[:ROWS] = queries_ref[...]
    place(x_at, c_at, mine_ref[0])
    place(x_at, 1 - c_at, mine_ref[1])
    for step in range(1, X):
        got_ref = got_refs[step - 1]
        blocks_ref[step * ROWS : (step + 1) * ROWS] = got_ref[:, :D]
        asking_ref[(X - step) * ROWS : (X - step + 1) * ROWS] = got_ref[:, D : 2 * D]
        x_from = (x_at + X - step) % X
        place(x_from, c_at, got_ref[:, 2 * D : 2 * D + D // X])
        place(x_from, 1 - c_at, got_ref[:, 2 * D + D // X :])
    scores_ref[...] = dot(queries_ref[...], blocks_ref[...], (1, 1)) * (D**-0.5)


def gather_kernel(parts_ref, out_ref):
    total = parts_ref[0].astype(F32)
    for at in range(1, Z_HI * Y):
        total = total + parts_ref[at].astype(F32)
    total = total.astype(BF16)
    for to in range(Y * Z_LO * CORE):
        out_ref[to] = total


def part_kernel(states_ref, grads_ref, asking_ref, *refs):
    *piece_refs, part_ref, passage_ref = refs
    part_ref[...] = dot(states_ref[...], grads_ref[...], (0, 0)).astype(BF16)
    pieces = jnp.concatenate([ref[...] for ref in piece_refs], axis=0)
    passage_ref[...] = (D**-0.5 * dot(pieces, asking_ref[...], (0, 0))).astype(BF16)


def around(x, axis, by):
    count = lax.axis_size(axis)
    return lax.ppermute(x, axis, [(i, (i + by) % count) for i in range(count)])


def swap(x, axis):
    return lax.all_to_all(x, axis, split_axis=0, concat_axis=0, tiled=True)


def local(query_states, passages, proj_weight, neg_store, positive, neg_owner, neg_slot, neg_count):
    factor = D**-0.5
    states = query_states.reshape(ROWS, D)
    own = passages.reshape(ROWS, D)
    store = neg_store.reshape(-1, D)
    place = jnp.stack([lax.axis_index("x"), lax.axis_index("c")]).astype(jnp.int32)

    request, mask = call(
        plan_kernel,
        (
            jax.ShapeDtypeStruct((MEMBERS, 1, CAP), jnp.int32),
            jax.ShapeDtypeStruct((ROWS, SLOTS), BF16),
        ),
        moved=1 << 20,
    )(neg_owner.reshape(ROWS, NEG), neg_slot.reshape(ROWS, NEG), neg_count.reshape(ROWS, 1))
    incoming = swap(request, BLK)

    queries = jnp.dot(states, proj_weight, preferred_element_type=F32).astype(BF16)
    below = around(own, "zh", 1)
    above = around(queries, "zh", -1)
    pair = around(states, "c", 1)
    incoming, below, above, pair = lax.optimization_barrier((incoming, below, above, pair))
    served = call(
        serve_kernel,
        jax.ShapeDtypeStruct((MEMBERS, CAP, D), BF16),
        flops=2 * SLOTS * store.shape[0] * D,
        moved=3 << 20,
    )(incoming, store)
    replies = swap(served, BLK).reshape(SLOTS, D)

    wide = jax.ShapeDtypeStruct((ROWS, 2 * D + CORE * (D // X)), BF16)
    *sends, mine = call(
        pack_kernel,
        (wide,) * (X - 1) + (jax.ShapeDtypeStruct((CORE, ROWS, D // X), BF16),),
        scalars=1,
        moved=6 << 20,
    )(place, own, below, queries, above, states, pair)
    got = [around(send, "x", step + 1) for step, send in enumerate(sends)]
    blocks, asking, row_states, scores = call(
        scores_kernel,
        (
            jax.ShapeDtypeStruct((STOPS * ROWS, D), BF16),
            jax.ShapeDtypeStruct((STOPS * ROWS, D), BF16),
            jax.ShapeDtypeStruct((X * CORE * ROWS, D // X), BF16),
            jax.ShapeDtypeStruct((ROWS, STOPS * ROWS), F32),
        ),
        scalars=1,
        flops=2 * ROWS * D * STOPS * ROWS,
        moved=6 << 20,
    )(place, own, queries, mine, *got)

    batch_grad, query_grad, halves = call(
        attend_kernel,
        (
            jax.ShapeDtypeStruct((ROWS, STOPS * ROWS), BF16),
            jax.ShapeDtypeStruct((ROWS, D), BF16),
            jax.ShapeDtypeStruct((X * CORE, ROWS, D // CORE), BF16),
        ),
        flops=2 * ROWS * D * (2 * SLOTS + STOPS * ROWS),
        moved=4 << 20,
    )(queries, scores, mask, positive.reshape(ROWS, 1), blocks, replies)
    row_grads = swap(halves, ("x", "c")).reshape(X * CORE * ROWS, D // CORE)

    pieces = [batch_grad[:, :ROWS]]
    for stop in range(1, STOPS):
        piece = batch_grad[:, stop * ROWS : (stop + 1) * ROWS]
        pieces.append(
            lax.ppermute(piece, BLK, [(i, (i - stop) % MEMBERS) for i in range(MEMBERS)])
        )
    part, passage_grads = call(
        part_kernel,
        (
            jax.ShapeDtypeStruct((D // X, D // CORE), BF16),
            jax.ShapeDtypeStruct((ROWS, D), BF16),
        ),
        flops=2 * ROWS * D * (STOPS * ROWS + D),
        moved=4 << 20,
    )(row_states, row_grads, asking, *pieces)
    state_grads = dot(query_grad, proj_weight, (1, 1))

    part = swap(part.reshape(Z_HI * Y, D // MEMBERS // Y, D // CORE), ("zh", "y"))
    part = call(
        gather_kernel,
        jax.ShapeDtypeStruct((Y * Z_LO * CORE,) + part.shape[1:], BF16),
        moved=1 << 20,
    )(part)
    parts = swap(part, GRP).reshape(Y, Z_LO, CORE, D // MEMBERS // Y, D // CORE)
    weight_grad = jnp.sum(parts.astype(F32), axis=1).transpose(0, 2, 1, 3)
    return (
        state_grads.astype(BF16).reshape(query_states.shape),
        passage_grads.reshape(passages.shape),
        weight_grad.reshape(D // MEMBERS, D),
    )


def solution(mesh):
    fine = Mesh(mesh.devices.reshape(Z_HI, X, Y, Z_LO, CORE), ("zh", "x", "y", "zl", "c"))
    placed = (
        P(BLK, GRP, None, None),
        P(BLK, GRP, None, None),
        P(),
        P(BLK, GRP, None, None),
        P(BLK, GRP, None),
        P(BLK, GRP, None, None),
        P(BLK, GRP, None, None),
        P(BLK, GRP, None),
    )
    return jax.shard_map(
        local,
        mesh=fine,
        in_specs=placed,
        out_specs=(P(BLK, GRP, None, None), P(BLK, GRP, None, None), P(BLK, None)),
        check_vma=False,
    )
```

```python
import jax
import jax.numpy as jnp
from jax import lax
from jax.experimental import pallas as pl
from jax.experimental.pallas import tpu as pltpu
from jax.sharding import Mesh, PartitionSpec as P

STOPS = 4
NEG = 7
CAP = 64
ROWS = 128
D = 1024
Z_HI, X, Y, Z_LO, CORE = 4, 4, 8, 3, 2
MEMBERS = Z_HI * X
SLOTS = MEMBERS * CAP
BLK = ("zh", "x")
GRP = ("y", "zl", "c")
F32 = jnp.float32
BF16 = jnp.bfloat16
LARGE = 58
PARTS = 4


def whole(x):
    return pl.BlockSpec(x.shape, lambda i, rank=len(x.shape): (0,) * rank)


def call(kernel, out_shape, *, scalars=0, flops=0, moved=0, limit=16, **kwargs):
    def run(*args):
        if "grid" not in kwargs:
            specs = [pl.BlockSpec(memory_space=pltpu.SMEM)] * scalars
            specs += [whole(arg) for arg in args[scalars:]]
            outs = jax.tree.map(whole, out_shape)
            spec = {"grid": (1,), "in_specs": specs, "out_specs": outs} | kwargs
        else:
            spec = kwargs
        return pl.pallas_call(
            kernel,
            out_shape=out_shape,
            compiler_params=pltpu.CompilerParams(vmem_limit_bytes=limit * 1024 * 1024),
            cost_estimate=pl.CostEstimate(flops=flops, bytes_accessed=moved, transcendentals=0),
            **spec,
        )(*args)

    return run


def dot(left, right, on):
    return lax.dot_general(left, right, ((on[:1], on[1:]), ((), ())), preferred_element_type=F32)


def plan_kernel(owner_ref, slot_ref, count_ref, request_ref, used_ref):
    lanes = ROWS
    row8 = lax.broadcasted_iota(jnp.int32, (8, lanes), 0)
    lane8 = lax.broadcasted_iota(jnp.int32, (8, lanes), 1)
    row = lax.broadcasted_iota(jnp.int32, (lanes, lanes), 0)
    lane = lax.broadcasted_iota(jnp.int32, (lanes, lanes), 1)

    def bits(value):
        return value.astype(F32).astype(BF16)

    owner = jnp.zeros((8, lanes), F32)
    for at in range(NEG):
        flat = owner_ref[at : at + 1, :]
        kept = jnp.where((lane8 + at * lanes) % NEG == row8, flat, 0)
        owner = owner + dot(bits(kept), bits((row + at * lanes) // NEG == lane), (1, 0))
    owner = jnp.where(row8 < NEG, owner.astype(jnp.int32), -1)
    named = (jnp.concatenate([owner] * MEMBERS, axis=0) == row // 8).astype(F32)
    before = dot(bits(named), bits(row < lane), (1, 0))
    above = bits((row // 8 == lane // 8) & (row > lane))
    base = jnp.sum(dot(above, bits(named), (1, 0)), axis=1, keepdims=True)
    place = named * (before + base + (row // 8 * CAP).astype(F32))
    placed = place[:8]
    for at in range(1, MEMBERS):
        placed = placed + place[at * 8 : (at + 1) * 8]
    placed = placed.astype(jnp.int32)
    slot = slot_ref[...]
    live = (row8 < count_ref[...]).astype(F32)
    column = lax.broadcasted_iota(jnp.int32, (SLOTS, lanes), 0)
    wanted = jnp.zeros((SLOTS, lanes), jnp.int32)
    used = jnp.zeros((SLOTS, lanes), F32)
    for j in range(NEG):
        match = column == placed[j : j + 1]
        wanted = wanted + jnp.where(match, slot[j : j + 1], 0)
        used = used + jnp.where(match, live[j : j + 1], 0.0)
    used_ref[...] = used.astype(BF16)
    ones = jnp.ones((8, lanes), BF16)
    high = dot(ones, bits(wanted // 256), (1, 1))[:1]
    low = dot(ones, bits(wanted % 256), (1, 1))[:1]
    request = (high * 256.0 + low).astype(jnp.int32)
    for owner_at in range(MEMBERS):
        request_ref[owner_at] = request[:, owner_at * CAP : (owner_at + 1) * CAP]


def serve_kernel(incoming_ref, store_ref, served_hbm, rows_ref, sems):
    pool = store_ref.shape[0]
    group = MEMBERS // PARTS
    row = lax.broadcasted_iota(jnp.int32, (pool, group * CAP), 0)
    sends = []
    for at in range(PARTS):
        wanted = [incoming_ref[at * group + k] for k in range(group)]
        pick = (row == jnp.concatenate(wanted, axis=1)).astype(F32).astype(BF16)
        rows = dot(pick, store_ref[...], (0, 0)).astype(BF16)
        rows_ref[at] = rows.reshape(group, CAP, D)
        target = served_hbm.at[pl.ds(at * group, group)]
        sends.append(pltpu.make_async_copy(rows_ref.at[at], target, sems.at[at]))
        sends[-1].start()
    for send in sends:
        send.wait()


def attend_kernel(
    queries_ref,
    scores_ref,
    mask_ref,
    positive_ref,
    blocks_ref,
    replies_ref,
    batch_ref,
    query_ref,
    halves_ref,
):
    factor = D**-0.5
    batch_scores = scores_ref[...]
    neg_scores = dot(queries_ref[...], replies_ref[...], (1, 1)) * factor
    neg_scores = jnp.where(mask_ref[...].astype(F32) > 0.5, neg_scores, -jnp.inf)
    top = jnp.maximum(
        jnp.max(batch_scores, axis=1, keepdims=True), jnp.max(neg_scores, axis=1, keepdims=True)
    )
    batch_exp = jnp.exp(batch_scores - top)
    neg_exp = jnp.exp(neg_scores - top)
    total = jnp.sum(batch_exp, axis=1, keepdims=True) + jnp.sum(neg_exp, axis=1, keepdims=True)
    column = lax.broadcasted_iota(jnp.int32, (ROWS, STOPS * ROWS), 1)
    hit = (column == positive_ref[...]).astype(F32)
    batch_grad = (batch_exp / total - hit).astype(BF16)
    neg_grad = (neg_exp / total).astype(BF16)
    batch_ref[...] = batch_grad
    inner = dot(batch_grad, blocks_ref[...], (1, 0)) + dot(neg_grad, replies_ref[...], (1, 0))
    query_grad = (factor * inner).astype(BF16)
    query_ref[...] = query_grad
    for to in range(X * CORE):
        at = to % CORE * (D // CORE)
        halves_ref[to] = query_grad[:, at : at + D // CORE]


def pack_kernel(place_ref, own_ref, below_ref, above_ref, states_ref, *refs):
    x_at = place_ref[0]
    share = D // MEMBERS

    def columns(x_to):
        piece = None
        for x_of in range(X):
            cut = [states_ref[:, (z * X + x_of) * share :][:, :share] for z in range(Z_HI)]
            cut = jnp.concatenate(cut, axis=1)
            piece = cut if piece is None else jnp.where(x_to == x_of, cut, piece)
        return piece

    *send_refs, mine_ref = refs
    mine_ref[...] = columns(x_at)
    for step in range(1, X):
        send_ref = send_refs[step - 1]
        wraps = x_at + step >= X
        send_ref[:, :D] = jnp.where(wraps, below_ref[...], own_ref[...])
        send_ref[:, D : 2 * D] = jnp.where(wraps, states_ref[...], above_ref[...])
        send_ref[:, 2 * D :] = columns((x_at + step) % X)


def unpack_kernel(place_ref, own_ref, states_ref, mine_ref, *refs):
    *got_refs, blocks_ref, asking_ref, row_ref = refs
    x_at = place_ref[0]
    blocks_ref[:ROWS] = own_ref[...]
    asking_ref[:ROWS] = states_ref[...]
    row_ref[x_at] = mine_ref[...]
    for step in range(1, X):
        got_ref = got_refs[step - 1]
        blocks_ref[step * ROWS : (step + 1) * ROWS] = got_ref[:, :D]
        asking_ref[(X - step) * ROWS : (X - step + 1) * ROWS] = got_ref[:, D : 2 * D]
        row_ref[(x_at + X - step) % X] = got_ref[:, 2 * D :]


def gather_kernel(parts_ref, out_ref):
    total = parts_ref[0].astype(F32)
    for at in range(1, Z_HI * Y):
        total = total + parts_ref[at].astype(F32)
    total = total.astype(BF16)
    for to in range(Y * Z_LO * CORE):
        out_ref[to] = total


def part_kernel(place_ref, states_ref, pair_ref, grads_ref, part_ref, total_ref):
    at = pl.program_id(0)
    c_at = place_ref[1]
    states = jnp.concatenate([states_ref[0], pair_ref[0]], axis=0)
    grads = jnp.concatenate([grads_ref[c_at], grads_ref[1 - c_at]], axis=0)
    term = dot(states, grads, (0, 0))

    @pl.when(at == 0)
    def _():
        total_ref[...] = term

    @pl.when(at > 0)
    def _():
        total_ref[...] += term

    @pl.when(at == pl.num_programs(0) - 1)
    def _():
        part_ref[...] = total_ref[...].astype(BF16)


def passage_kernel(asking_ref, *refs):
    *piece_refs, passage_ref = refs
    pieces = jnp.concatenate([ref[...] for ref in piece_refs], axis=0)
    passage_ref[...] = (D**-0.5 * dot(pieces, asking_ref[...], (0, 0))).astype(BF16)


def around(x, axis, by):
    count = lax.axis_size(axis)
    return lax.ppermute(x, axis, [(i, (i + by) % count) for i in range(count)])


def swap(x, axis):
    return lax.all_to_all(x, axis, split_axis=0, concat_axis=0, tiled=True)


def local(query_states, passages, proj_weight, neg_store, positive, neg_owner, neg_slot, neg_count):
    factor = D**-0.5
    states = query_states.reshape(ROWS, D)
    own = passages.reshape(ROWS, D)
    store = neg_store.reshape(-1, D)
    place = jnp.stack([lax.axis_index(axis) for axis in ("x", "c", "zh")]).astype(jnp.int32)

    request, used = call(
        plan_kernel,
        (
            jax.ShapeDtypeStruct((MEMBERS, 1, CAP), jnp.int32),
            jax.ShapeDtypeStruct((SLOTS, ROWS), BF16),
        ),
        moved=1 << 20,
    )(neg_owner.reshape(NEG, ROWS), neg_slot.reshape(ROWS, NEG).T, neg_count.reshape(1, ROWS))
    mask = used.T
    incoming = swap(request, BLK)

    below = around(own, "zh", 1)
    above = around(states, "zh", -1)
    incoming = lax.optimization_barrier((incoming, below, above))[0]
    served = call(
        serve_kernel,
        jax.ShapeDtypeStruct((MEMBERS, CAP, D), BF16),
        flops=2 * SLOTS * store.shape[0] * D,
        moved=3 << 20,
        limit=LARGE,
        grid=(1,),
        in_specs=[
            pl.BlockSpec((MEMBERS, 1, CAP), lambda i: (0, 0, 0)),
            pl.BlockSpec(store.shape, lambda i: (0, 0)),
        ],
        out_specs=pl.BlockSpec(memory_space=pltpu.HBM),
        scratch_shapes=[
            pltpu.VMEM((PARTS, MEMBERS // PARTS, CAP, D), BF16),
            pltpu.SemaphoreType.DMA((PARTS,)),
        ],
    )(incoming, store)
    replies = swap(served, BLK).reshape(SLOTS, D)

    wide = jax.ShapeDtypeStruct((ROWS, 2 * D + D // X), BF16)
    *sends, mine = call(
        pack_kernel,
        (wide,) * (X - 1) + (jax.ShapeDtypeStruct((ROWS, D // X), BF16),),
        scalars=1,
        moved=6 << 20,
    )(place, own, below, above, states)
    got = [around(send, "x", step + 1) for step, send in enumerate(sends)]
    blocks, asking, row_states = call(
        unpack_kernel,
        (
            jax.ShapeDtypeStruct((STOPS * ROWS, D), BF16),
            jax.ShapeDtypeStruct((STOPS * ROWS, D), BF16),
            jax.ShapeDtypeStruct((X, ROWS, D // X), BF16),
        ),
        scalars=1,
        moved=6 << 20,
    )(place, own, states, mine, *got)
    pair_states = around(row_states, "c", 1)
    asking = jnp.dot(asking, proj_weight, preferred_element_type=F32).astype(BF16)
    queries = asking[:ROWS]
    scores = dot(queries, blocks, (1, 1)) * factor
    batch_grad, query_grad, halves = call(
        attend_kernel,
        (
            jax.ShapeDtypeStruct((ROWS, STOPS * ROWS), BF16),
            jax.ShapeDtypeStruct((ROWS, D), BF16),
            jax.ShapeDtypeStruct((X * CORE, ROWS, D // CORE), BF16),
        ),
        limit=LARGE,
        flops=2 * ROWS * D * (2 * SLOTS + STOPS * ROWS),
        moved=4 << 20,
    )(queries, scores, mask, positive.reshape(ROWS, 1), blocks, replies)
    row_grads = swap(halves, ("x", "c"))

    def to_owner(stop, batch):
        piece = batch[:, stop * ROWS : (stop + 1) * ROWS]
        return lax.ppermute(piece, BLK, [(i, (i - stop) % MEMBERS) for i in range(MEMBERS)])

    pieces = [batch_grad[:, :ROWS], to_owner(1, batch_grad)]
    row_grads = lax.optimization_barrier((row_grads, pieces[1]))[0]
    part = call(
        part_kernel,
        jax.ShapeDtypeStruct((D // X, D // CORE), BF16),
        limit=LARGE,
        flops=2 * ROWS * D * D,
        moved=2 << 20,
        grid=(X,),
        in_specs=[
            pl.BlockSpec(memory_space=pltpu.SMEM),
            pl.BlockSpec((1, ROWS, D // X), lambda i: (i, 0, 0)),
            pl.BlockSpec((1, ROWS, D // X), lambda i: (i, 0, 0)),
            pl.BlockSpec((CORE, ROWS, D // CORE), lambda i: (i, 0, 0)),
        ],
        out_specs=pl.BlockSpec((D // X, D // CORE), lambda i: (0, 0)),
        scratch_shapes=[pltpu.VMEM((D // X, D // CORE), F32)],
    )(place, row_states, pair_states, row_grads)
    pieces.append(to_owner(2, lax.optimization_barrier((batch_grad, part))[0]))
    state_grads = dot(query_grad, proj_weight, (1, 1))

    part = swap(part.reshape(Z_HI * Y, D // MEMBERS // Y, D // CORE), ("zh", "y"))
    part = lax.optimization_barrier((part, pieces[2]))[0]
    part = call(
        gather_kernel,
        jax.ShapeDtypeStruct((Y * Z_LO * CORE,) + part.shape[1:], BF16),
        limit=LARGE,
        moved=1 << 20,
    )(part)
    pieces.append(to_owner(3, lax.optimization_barrier((batch_grad, part))[0]))
    passage_grads = call(
        passage_kernel,
        jax.ShapeDtypeStruct((ROWS, D), BF16),
        flops=2 * ROWS * D * STOPS * ROWS,
        moved=2 << 20,
    )(asking, *pieces)

    parts = swap(part, GRP).reshape(Y, Z_LO, CORE, D // MEMBERS // Y, D // CORE)
    weight_grad = jnp.sum(parts.astype(F32), axis=1).transpose(0, 2, 1, 3)
    return (
        state_grads.astype(BF16).reshape(query_states.shape),
        passage_grads.reshape(passages.shape),
        weight_grad.reshape(D // MEMBERS, D),
    )


def solution(mesh):
    fine = Mesh(mesh.devices.reshape(Z_HI, X, Y, Z_LO, CORE), ("zh", "x", "y", "zl", "c"))
    placed = (
        P(BLK, GRP, None, None),
        P(BLK, GRP, None, None),
        P(),
        P(BLK, GRP, None, None),
        P(BLK, GRP, None),
        P(BLK, GRP, None, None),
        P(BLK, GRP, None, None),
        P(BLK, GRP, None),
    )
    return jax.shard_map(
        local,
        mesh=fine,
        in_specs=placed,
        out_specs=(P(BLK, GRP, None, None), P(BLK, GRP, None, None), P(BLK, None)),
        check_vma=False,
    )
```

```python
import jax
import jax.numpy as jnp
from jax import lax
from jax.experimental import pallas as pl
from jax.experimental.pallas import tpu as pltpu
from jax.sharding import Mesh, PartitionSpec as P

STOPS = 4
NEG = 7
CAP = 64
ROWS = 128
D = 1024
Z_HI, X, Y_HI, Y_LO, Z_LO, CORE = 4, 4, 4, 2, 3, 2
QUARTERS = Y_LO * CORE
MEMBERS = Z_HI * X
SLOTS = MEMBERS * CAP
BLK = ("zh", "x")
GRP = ("yh", "yl", "zl", "c")
F32 = jnp.float32
BF16 = jnp.bfloat16
LARGE = 58
STAT_ROWS = 16
PARTS = 4


def whole(x):
    return pl.BlockSpec(x.shape, lambda i, rank=len(x.shape): (0,) * rank)


def call(kernel, out_shape, *, scalars=0, flops=0, moved=0, limit=16, **kwargs):
    def run(*args):
        if "grid" not in kwargs:
            specs = [pl.BlockSpec(memory_space=pltpu.SMEM)] * scalars
            specs += [whole(arg) for arg in args[scalars:]]
            outs = jax.tree.map(whole, out_shape)
            spec = {"grid": (1,), "in_specs": specs, "out_specs": outs} | kwargs
        else:
            spec = kwargs
        return pl.pallas_call(
            kernel,
            out_shape=out_shape,
            compiler_params=pltpu.CompilerParams(vmem_limit_bytes=limit * 1024 * 1024),
            cost_estimate=pl.CostEstimate(flops=flops, bytes_accessed=moved, transcendentals=0),
            **spec,
        )(*args)

    return run


def dot(left, right, on):
    return lax.dot_general(left, right, ((on[:1], on[1:]), ((), ())), preferred_element_type=F32)


def plan_kernel(owner_ref, slot_ref, count_ref, request_ref, used_ref):
    lanes = ROWS
    row8 = lax.broadcasted_iota(jnp.int32, (8, lanes), 0)
    lane8 = lax.broadcasted_iota(jnp.int32, (8, lanes), 1)
    row = lax.broadcasted_iota(jnp.int32, (lanes, lanes), 0)
    lane = lax.broadcasted_iota(jnp.int32, (lanes, lanes), 1)

    def bits(value):
        return value.astype(F32).astype(BF16)

    owner = jnp.zeros((8, lanes), F32)
    for at in range(NEG):
        flat = owner_ref[at]
        kept = jnp.where((lane8 + at * lanes) % NEG == row8, flat, 0)
        owner = owner + dot(bits(kept), bits((row + at * lanes) // NEG == lane), (1, 0))
    owner = jnp.where(row8 < NEG, owner.astype(jnp.int32), -1)
    named = (jnp.concatenate([owner] * MEMBERS, axis=0) == row // 8).astype(F32)
    before = dot(bits(named), bits(row < lane), (1, 0))
    above = bits((row // 8 == lane // 8) & (row > lane))
    base = jnp.sum(dot(above, bits(named), (1, 0)), axis=1, keepdims=True)
    place = named * (before + base + (row // 8 * CAP).astype(F32))
    placed = place[:8]
    for at in range(1, MEMBERS):
        placed = placed + place[at * 8 : (at + 1) * 8]
    placed = placed.astype(jnp.int32)
    live = (row8 < count_ref[0]).astype(F32)
    column = lax.broadcasted_iota(jnp.int32, (SLOTS, lanes), 0)
    wanted = jnp.zeros((SLOTS, lanes), jnp.int32)
    used = jnp.zeros((SLOTS, lanes), F32)
    for j in range(NEG):
        match = column == placed[j : j + 1]
        wanted = wanted + jnp.where(match, slot_ref[j], 0)
        used = used + jnp.where(match, live[j : j + 1], 0.0)
    used_ref[...] = used.astype(BF16)
    ones = jnp.ones((8, lanes), BF16)
    high = dot(ones, bits(wanted // 256), (1, 1))[:1]
    low = dot(ones, bits(wanted % 256), (1, 1))[:1]
    request = (high * 256.0 + low).astype(jnp.int32)
    for owner_at in range(MEMBERS):
        request_ref[owner_at] = request[:, owner_at * CAP : (owner_at + 1) * CAP]


def serve_kernel(incoming_ref, store_ref, served_hbm, rows_ref, sems):
    pool = store_ref.shape[0]
    group = MEMBERS // PARTS
    row = lax.broadcasted_iota(jnp.int32, (pool, group * CAP), 0)
    sends = []
    for at in range(PARTS):
        wanted = [incoming_ref[at * group + k] for k in range(group)]
        pick = (row == jnp.concatenate(wanted, axis=1)).astype(F32).astype(BF16)
        rows = dot(pick, store_ref[...], (0, 0)).astype(BF16)
        rows_ref[at] = rows.reshape(group, CAP, D)
        target = served_hbm.at[pl.ds(at * group, group)]
        sends.append(pltpu.make_async_copy(rows_ref.at[at], target, sems.at[at]))
        sends[-1].start()
    for send in sends:
        send.wait()


def in_three(value):
    first = value.astype(BF16).astype(F32)
    second = (value - first).astype(BF16).astype(F32)
    return first, second, value - first - second


def attend_kernel(
    queries_ref, scores_ref, mask_ref, positive_ref, blocks_ref, replies_ref, query_ref, quarters_ref
):
    factor = D**-0.5
    batch_scores = scores_ref[...]
    neg_scores = dot(queries_ref[...], replies_ref[...], (1, 1)) * factor
    neg_scores = jnp.where(mask_ref[...].astype(F32) > 0.5, neg_scores, -jnp.inf)
    top = jnp.maximum(
        jnp.max(batch_scores, axis=1, keepdims=True), jnp.max(neg_scores, axis=1, keepdims=True)
    )
    batch_exp = jnp.exp(batch_scores - top)
    neg_exp = jnp.exp(neg_scores - top)
    total = jnp.sum(batch_exp, axis=1, keepdims=True) + jnp.sum(neg_exp, axis=1, keepdims=True)
    column = lax.broadcasted_iota(jnp.int32, (ROWS, STOPS * ROWS), 1)
    hit = (column == positive_ref[...]).astype(F32)
    batch_grad = (batch_exp / total - hit).astype(BF16)
    neg_grad = (neg_exp / total).astype(BF16)
    inner = dot(batch_grad, blocks_ref[...], (1, 0)) + dot(neg_grad, replies_ref[...], (1, 0))
    query_grad = (factor * inner).astype(BF16)
    query_ref[...] = query_grad

    lane = lax.broadcasted_iota(jnp.int32, (ROWS, ROWS), 1)
    row = lax.broadcasted_iota(jnp.int32, (ROWS, ROWS), 0)
    stats = jnp.zeros((ROWS, ROWS), F32)
    for at, value in enumerate(in_three(top) + in_three(total)):
        stats = jnp.where(lane == at, value, stats)
    turned = dot(stats.astype(BF16), (lane == row).astype(F32).astype(BF16), (0, 0))
    turned = turned[:STAT_ROWS].astype(BF16)
    rest = jnp.zeros((STAT_ROWS, D // QUARTERS - ROWS), BF16)
    turned = jnp.concatenate([turned, rest], axis=1)
    for to in range(X * QUARTERS):
        at = to % QUARTERS * (D // QUARTERS)
        quarters_ref[to, :ROWS] = query_grad[:, at : at + D // QUARTERS]
        quarters_ref[to, ROWS:] = turned


def pack_kernel(place_ref, own_ref, below_ref, above_ref, states_ref, *refs):
    x_at = place_ref[0]
    share = D // MEMBERS

    def columns(x_to):
        piece = None
        for x_of in range(X):
            cut = [states_ref[:, (z * X + x_of) * share :][:, :share] for z in range(Z_HI)]
            cut = jnp.concatenate(cut, axis=1)
            piece = cut if piece is None else jnp.where(x_to == x_of, cut, piece)
        return piece

    first_refs, second_refs, mine_ref = refs[: X - 1], refs[X - 1 : 2 * X - 2], refs[-1]
    mine_ref[...] = columns(x_at)
    for step in range(1, X):
        wraps = x_at + step >= X
        first_ref, second_ref = first_refs[step - 1], second_refs[step - 1]
        first_ref[:, :D] = jnp.where(wraps, below_ref[...], own_ref[...])
        first_ref[:, D:] = columns((x_at + step) % X)
        second_ref[...] = jnp.where(wraps, states_ref[...], above_ref[...])


def unpack_kernel(place_ref, own_ref, mine_ref, *refs):
    *got_refs, blocks_ref, row_ref = refs
    x_at = place_ref[0]
    blocks_ref[:ROWS] = own_ref[...]
    row_ref[x_at] = mine_ref[...]
    for step in range(1, X):
        got_ref = got_refs[step - 1]
        blocks_ref[step * ROWS : (step + 1) * ROWS] = got_ref[:, :D]
        row_ref[(x_at + X - step) % X] = got_ref[:, D:]


def gather_kernel(parts_ref, out_ref):
    total = parts_ref[0].astype(F32)
    for at in range(1, Z_HI * Y_HI):
        total = total + parts_ref[at].astype(F32)
    total = total.astype(BF16)
    for to in range(Y_HI * Y_LO * Z_LO * CORE):
        out_ref[to] = total


def asking_kernel(weight_ref, own_ref, *refs):
    *states_refs, queries_ref, scores_ref = refs
    states = jnp.concatenate([ref[...] for ref in states_refs], axis=0)
    queries = dot(states, weight_ref[...], (1, 0)).astype(BF16)
    queries_ref[...] = queries
    scores_ref[...] = dot(own_ref[...], queries, (1, 1)) * (D**-0.5)


def part_kernel(place_ref, states_ref, pair_ref, grads_ref, part_ref, stats_ref, total_ref):
    at = pl.program_id(0)
    c_at, y_at = place_ref[1], place_ref[3]
    states = [states_ref[0, 0], states_ref[1, 0], pair_ref[0, 0], pair_ref[1, 0]]
    mine, other = y_at * CORE, (1 - y_at) * CORE
    froms = [mine + c_at, other + c_at, mine + 1 - c_at, other + 1 - c_at]
    grads = [grads_ref[source, :ROWS] for source in froms]
    term = dot(jnp.concatenate(states, axis=0), jnp.concatenate(grads, axis=0), (0, 0))
    stats_ref[at] = grads_ref[mine + c_at, ROWS:, :ROWS]

    @pl.when(at == 0)
    def _():
        total_ref[...] = term

    @pl.when(at > 0)
    def _():
        total_ref[...] += term

    @pl.when(at == pl.num_programs(0) - 1)
    def _():
        part_ref[...] = total_ref[...].astype(BF16)


def passage_kernel(
    place_ref, scores_ref, queries_ref, stats_ref, upper_ref, positive_ref, passage_ref
):
    x_at = place_ref[0]
    row = lax.broadcasted_iota(jnp.int32, (ROWS, ROWS), 0)
    total = jnp.zeros((ROWS, D), F32)
    for stop in range(STOPS):
        x_from = x_at + stop
        here = stats_ref[x_from % X].astype(F32)
        stats = jnp.where(x_from < X, here, upper_ref[x_from % X].astype(F32))
        top = stats[0:1] + stats[1:2] + stats[2:3]
        weight = stats[3:4] + stats[4:5] + stats[5:6]
        cut = slice(stop * ROWS, (stop + 1) * ROWS)
        grad = jnp.exp(scores_ref[:, cut] - top) / weight
        if stop == 0:
            grad = grad - (row == positive_ref[...]).astype(F32)
        total = total + dot(grad.astype(BF16), queries_ref[cut], (1, 0))
    passage_ref[...] = (D**-0.5 * total).astype(BF16)


def finish_kernel(parts_ref, out_ref):
    height = D // MEMBERS // Y_HI
    for y_hi in range(Y_HI):
        for quarter in range(QUARTERS):
            y_lo, c_of = quarter // CORE, quarter % CORE
            total = None
            for z_lo in range(Z_LO):
                block = parts_ref[((y_hi * Y_LO + y_lo) * Z_LO + z_lo) * CORE + c_of].astype(F32)
                total = block if total is None else total + block
            rows = slice(y_hi * height, (y_hi + 1) * height)
            out_ref[rows, quarter * (D // QUARTERS) : (quarter + 1) * (D // QUARTERS)] = total


def around(x, axis, by):
    count = lax.axis_size(axis)
    return lax.ppermute(x, axis, [(i, (i + by) % count) for i in range(count)])


def swap(x, axis):
    return lax.all_to_all(x, axis, split_axis=0, concat_axis=0, tiled=True)


def local(query_states, passages, proj_weight, neg_store, positive, neg_owner, neg_slot, neg_count):
    factor = D**-0.5
    states = query_states.reshape(ROWS, D)
    own = passages.reshape(ROWS, D)
    store = neg_store.reshape(-1, D)
    place = jnp.stack([lax.axis_index(axis) for axis in ("x", "c", "zh", "yl")]).astype(jnp.int32)

    request, used = call(
        plan_kernel,
        (
            jax.ShapeDtypeStruct((MEMBERS, 1, CAP), jnp.int32),
            jax.ShapeDtypeStruct((SLOTS, ROWS), BF16),
        ),
        limit=LARGE,
        moved=1 << 20,
    )(
        neg_owner.reshape(NEG, 1, ROWS),
        neg_slot.reshape(ROWS, NEG).T.reshape(NEG, 1, ROWS),
        neg_count.reshape(1, 1, ROWS),
    )
    mask = used.T
    incoming = swap(request, BLK)

    below = around(own, "zh", 1)
    above = around(states, "zh", -1)
    incoming = lax.optimization_barrier((incoming, below, above))[0]
    served = call(
        serve_kernel,
        jax.ShapeDtypeStruct((MEMBERS, CAP, D), BF16),
        flops=2 * SLOTS * store.shape[0] * D,
        moved=3 << 20,
        limit=LARGE,
        grid=(1,),
        in_specs=[
            pl.BlockSpec((MEMBERS, 1, CAP), lambda i: (0, 0, 0)),
            pl.BlockSpec(store.shape, lambda i: (0, 0)),
        ],
        out_specs=pl.BlockSpec(memory_space=pltpu.HBM),
        scratch_shapes=[
            pltpu.VMEM((PARTS, MEMBERS // PARTS, CAP, D), BF16),
            pltpu.SemaphoreType.DMA((PARTS,)),
        ],
    )(incoming, store)
    replies = swap(served, BLK).reshape(SLOTS, D)

    wide = jax.ShapeDtypeStruct((ROWS, D + D // X), BF16)
    sends = call(
        pack_kernel,
        (wide,) * (X - 1)
        + (jax.ShapeDtypeStruct((ROWS, D), BF16),) * (X - 1)
        + (jax.ShapeDtypeStruct((ROWS, D // X), BF16),),
        scalars=1,
        moved=6 << 20,
    )(place, own, below, above, states)
    mine = sends[-1]
    got = [around(send, "x", step + 1) for step, send in enumerate(sends[: X - 1])]
    blocks, row_states = call(
        unpack_kernel,
        (
            jax.ShapeDtypeStruct((STOPS * ROWS, D), BF16),
            jax.ShapeDtypeStruct((X, ROWS, D // X), BF16),
        ),
        scalars=1,
        moved=4 << 20,
    )(place, own, mine, *got)
    next_states = around(row_states, "yl", 1)
    row_states = jnp.stack([row_states, next_states])
    pair_states = around(row_states, "c", 1)
    late = lax.optimization_barrier((*sends[X - 1 : -1], *got))[: X - 1]
    late = [around(send, "x", step + 1) for step, send in enumerate(late)]
    asking, own_scores = call(
        asking_kernel,
        (
            jax.ShapeDtypeStruct((STOPS * ROWS, D), BF16),
            jax.ShapeDtypeStruct((ROWS, STOPS * ROWS), F32),
        ),
        flops=25 * 10**9,
        moved=4 << 20,
    )(proj_weight, own, states, *late[::-1])
    replies = lax.optimization_barrier((replies, pair_states, own_scores))[0]
    queries = jnp.dot(states, proj_weight, preferred_element_type=F32).astype(BF16)
    scores = dot(queries, blocks, (1, 1)) * factor

    query_grad, quarters = call(
        attend_kernel,
        (
            jax.ShapeDtypeStruct((ROWS, D), BF16),
            jax.ShapeDtypeStruct((X * QUARTERS, ROWS + STAT_ROWS, D // QUARTERS), BF16),
        ),
        limit=LARGE,
        flops=2 * ROWS * D * (2 * SLOTS + STOPS * ROWS),
        moved=4 << 20,
    )(queries, scores, mask, positive.reshape(ROWS, 1), blocks, replies)
    row_grads = swap(quarters, ("x", "yl", "c"))

    part, stats = call(
        part_kernel,
        (
            jax.ShapeDtypeStruct((D // X, D // QUARTERS), BF16),
            jax.ShapeDtypeStruct((X, STAT_ROWS, ROWS), BF16),
        ),
        limit=LARGE,
        flops=2 * ROWS * D * D,
        moved=2 << 20,
        grid=(X,),
        in_specs=[
            pl.BlockSpec(memory_space=pltpu.SMEM),
            pl.BlockSpec((Y_LO, 1, ROWS, D // X), lambda i: (0, i, 0, 0)),
            pl.BlockSpec((Y_LO, 1, ROWS, D // X), lambda i: (0, i, 0, 0)),
            pl.BlockSpec((QUARTERS, ROWS + STAT_ROWS, D // QUARTERS), lambda i: (i, 0, 0)),
        ],
        out_specs=[
            pl.BlockSpec((D // X, D // QUARTERS), lambda i: (0, 0)),
            pl.BlockSpec((X, STAT_ROWS, ROWS), lambda i: (0, 0, 0)),
        ],
        scratch_shapes=[pltpu.VMEM((D // X, D // QUARTERS), F32)],
    )(place, row_states, pair_states, row_grads)
    state_grads = dot(query_grad, proj_weight, (1, 1)).astype(BF16)

    height = D // MEMBERS // Y_HI
    part = swap(part.reshape(Z_HI * Y_HI, height, D // QUARTERS), ("zh", "yh"))
    upper = around(stats, "zh", -1)
    part, state_grads, upper = lax.optimization_barrier((part, state_grads, upper))
    part = call(
        gather_kernel,
        jax.ShapeDtypeStruct((Y_HI * Y_LO * Z_LO * CORE,) + part.shape[1:], BF16),
        limit=LARGE,
        moved=1 << 20,
    )(part)
    upper = lax.optimization_barrier((upper, part))[0]
    passage_grads = call(
        passage_kernel,
        jax.ShapeDtypeStruct((ROWS, D), BF16),
        scalars=1,
        flops=2 * ROWS * D * STOPS * ROWS,
        moved=2 << 20,
    )(place, own_scores, asking, stats, upper, positive.reshape(1, ROWS))

    weight_grad = call(
        finish_kernel,
        jax.ShapeDtypeStruct((D // MEMBERS, D), F32),
        limit=LARGE,
        moved=1 << 20,
    )(swap(part, GRP))
    return (
        state_grads.reshape(query_states.shape),
        passage_grads.reshape(passages.shape),
        weight_grad,
    )


def solution(mesh):
    shape = (Z_HI, X, Y_HI, Y_LO, Z_LO, CORE)
    fine = Mesh(mesh.devices.reshape(shape), ("zh", "x", "yh", "yl", "zl", "c"))
    placed = (
        P(BLK, GRP, None, None),
        P(BLK, GRP, None, None),
        P(),
        P(BLK, GRP, None, None),
        P(BLK, GRP, None),
        P(BLK, GRP, None, None),
        P(BLK, GRP, None, None),
        P(BLK, GRP, None),
    )
    return jax.shard_map(
        local,
        mesh=fine,
        in_specs=placed,
        out_specs=(P(BLK, GRP, None, None), P(BLK, GRP, None, None), P(BLK, None)),
        check_vma=False,
    )
```

```python
import jax
import jax.numpy as jnp
from jax import lax
from jax.experimental import pallas as pl
from jax.experimental.pallas import tpu as pltpu
from jax.sharding import Mesh, PartitionSpec as P

STOPS = 4
NEG = 7
CAP = 64
ROWS = 128
D = 1024
Z_HI, X, Y_HI, Y_LO, Z_LO, CORE = 4, 4, 4, 2, 3, 2
QUARTERS = Y_LO * CORE
MEMBERS = Z_HI * X
SLOTS = MEMBERS * CAP
BLK = ("zh", "x")
GRP = ("yh", "yl", "zl", "c")
F32 = jnp.float32
BF16 = jnp.bfloat16
LARGE = 58
STAT_ROWS = 16
PARTS = 4


def whole(x):
    return pl.BlockSpec(x.shape, lambda i, rank=len(x.shape): (0,) * rank)


def call(kernel, out_shape, *, scalars=0, flops=0, moved=0, limit=16, **kwargs):
    def run(*args):
        if "grid" not in kwargs:
            specs = [pl.BlockSpec(memory_space=pltpu.SMEM)] * scalars
            specs += [whole(arg) for arg in args[scalars:]]
            outs = jax.tree.map(whole, out_shape)
            spec = {"grid": (1,), "in_specs": specs, "out_specs": outs} | kwargs
        else:
            spec = kwargs
        return pl.pallas_call(
            kernel,
            out_shape=out_shape,
            compiler_params=pltpu.CompilerParams(vmem_limit_bytes=limit * 1024 * 1024),
            cost_estimate=pl.CostEstimate(flops=flops, bytes_accessed=moved, transcendentals=0),
            **spec,
        )(*args)

    return run


def dot(left, right, on):
    return lax.dot_general(left, right, ((on[:1], on[1:]), ((), ())), preferred_element_type=F32)


def plan_kernel(owner_ref, slot_ref, count_ref, request_ref, used_ref):
    lanes = ROWS
    row8 = lax.broadcasted_iota(jnp.int32, (8, lanes), 0)
    lane8 = lax.broadcasted_iota(jnp.int32, (8, lanes), 1)
    row = lax.broadcasted_iota(jnp.int32, (lanes, lanes), 0)
    lane = lax.broadcasted_iota(jnp.int32, (lanes, lanes), 1)

    def bits(value):
        return value.astype(F32).astype(BF16)

    owner = jnp.zeros((8, lanes), F32)
    for at in range(NEG):
        flat = owner_ref[at]
        kept = jnp.where((lane8 + at * lanes) % NEG == row8, flat, 0)
        owner = owner + dot(bits(kept), bits((row + at * lanes) // NEG == lane), (1, 0))
    owner = jnp.where(row8 < NEG, owner.astype(jnp.int32), -1)
    named = (jnp.concatenate([owner] * MEMBERS, axis=0) == row // 8).astype(F32)
    before = dot(bits(named), bits(row < lane), (1, 0))
    above = bits((row // 8 == lane // 8) & (row > lane))
    base = jnp.sum(dot(above, bits(named), (1, 0)), axis=1, keepdims=True)
    place = named * (before + base + (row // 8 * CAP).astype(F32))
    placed = place[:8]
    for at in range(1, MEMBERS):
        placed = placed + place[at * 8 : (at + 1) * 8]
    placed = placed.astype(jnp.int32)
    live = (row8 < count_ref[0]).astype(F32)
    column = lax.broadcasted_iota(jnp.int32, (SLOTS, lanes), 0)
    wanted = jnp.zeros((SLOTS, lanes), jnp.int32)
    used = jnp.zeros((SLOTS, lanes), F32)
    for j in range(NEG):
        match = column == placed[j : j + 1]
        wanted = wanted + jnp.where(match, slot_ref[j], 0)
        used = used + jnp.where(match, live[j : j + 1], 0.0)
    used_ref[...] = used.astype(BF16)
    ones = jnp.ones((8, lanes), BF16)
    high = dot(ones, bits(wanted // 256), (1, 1))[:1]
    low = dot(ones, bits(wanted % 256), (1, 1))[:1]
    request = (high * 256.0 + low).astype(jnp.int32)
    for owner_at in range(MEMBERS):
        request_ref[owner_at] = request[:, owner_at * CAP : (owner_at + 1) * CAP]


def serve_kernel(incoming_ref, store_ref, served_hbm, rows_ref, sems):
    pool = store_ref.shape[0]
    group = MEMBERS // PARTS
    row = lax.broadcasted_iota(jnp.int32, (pool, group * CAP), 0)
    sends = []
    for at in range(PARTS):
        wanted = [incoming_ref[at * group + k] for k in range(group)]
        pick = (row == jnp.concatenate(wanted, axis=1)).astype(F32).astype(BF16)
        rows = dot(pick, store_ref[...], (0, 0)).astype(BF16)
        rows_ref[at] = rows.reshape(group, CAP, D)
        target = served_hbm.at[pl.ds(at * group, group)]
        sends.append(pltpu.make_async_copy(rows_ref.at[at], target, sems.at[at]))
        sends[-1].start()
    for send in sends:
        send.wait()


def in_three(value):
    first = value.astype(BF16).astype(F32)
    second = (value - first).astype(BF16).astype(F32)
    return first, second, value - first - second


def attend_kernel(
    queries_ref, scores_ref, mask_ref, positive_ref, blocks_ref, replies_ref, query_ref, quarters_ref
):
    factor = D**-0.5
    batch_scores = scores_ref[...]
    neg_scores = dot(queries_ref[...], replies_ref[...], (1, 1)) * factor
    neg_scores = jnp.where(mask_ref[...].astype(F32) > 0.5, neg_scores, -jnp.inf)
    top = jnp.maximum(
        jnp.max(batch_scores, axis=1, keepdims=True), jnp.max(neg_scores, axis=1, keepdims=True)
    )
    batch_exp = jnp.exp(batch_scores - top)
    neg_exp = jnp.exp(neg_scores - top)
    total = jnp.sum(batch_exp, axis=1, keepdims=True) + jnp.sum(neg_exp, axis=1, keepdims=True)
    column = lax.broadcasted_iota(jnp.int32, (ROWS, STOPS * ROWS), 1)
    hit = (column == positive_ref[...]).astype(F32)
    batch_grad = (batch_exp / total - hit).astype(BF16)
    neg_grad = (neg_exp / total).astype(BF16)
    inner = dot(batch_grad, blocks_ref[...], (1, 0)) + dot(neg_grad, replies_ref[...], (1, 0))
    query_grad = (factor * inner).astype(BF16)
    query_ref[...] = query_grad

    lane = lax.broadcasted_iota(jnp.int32, (ROWS, ROWS), 1)
    row = lax.broadcasted_iota(jnp.int32, (ROWS, ROWS), 0)
    stats = jnp.zeros((ROWS, ROWS), F32)
    for at, value in enumerate(in_three(top) + in_three(total)):
        stats = jnp.where(lane == at, value, stats)
    turned = dot(stats.astype(BF16), (lane == row).astype(F32).astype(BF16), (0, 0))
    turned = turned[:STAT_ROWS].astype(BF16)
    rest = jnp.zeros((STAT_ROWS, D // QUARTERS - ROWS), BF16)
    turned = jnp.concatenate([turned, rest], axis=1)
    for to in range(X * QUARTERS):
        at = to % QUARTERS * (D // QUARTERS)
        quarters_ref[to, :ROWS] = query_grad[:, at : at + D // QUARTERS]
        quarters_ref[to, ROWS:] = turned


def pack_kernel(place_ref, own_ref, below_ref, above_ref, states_ref, *refs):
    x_at = place_ref[0]
    share = D // MEMBERS

    def columns(x_to):
        piece = None
        for x_of in range(X):
            cut = [states_ref[:, (z * X + x_of) * share :][:, :share] for z in range(Z_HI)]
            cut = jnp.concatenate(cut, axis=1)
            piece = cut if piece is None else jnp.where(x_to == x_of, cut, piece)
        return piece

    first_refs, second_refs, mine_ref = refs[: X - 1], refs[X - 1 : 2 * X - 2], refs[-1]
    mine_ref[...] = columns(x_at)
    for step in range(1, X):
        wraps = x_at + step >= X
        first_ref, second_ref = first_refs[step - 1], second_refs[step - 1]
        first_ref[:, :D] = jnp.where(wraps, below_ref[...], own_ref[...])
        first_ref[:, D:] = columns((x_at + step) % X)
        second_ref[...] = jnp.where(wraps, states_ref[...], above_ref[...])


def unpack_kernel(place_ref, own_ref, mine_ref, *refs):
    *got_refs, blocks_ref, row_ref = refs
    x_at = place_ref[0]
    blocks_ref[:ROWS] = own_ref[...]
    row_ref[x_at] = mine_ref[...].astype(F32).T.astype(BF16)
    for step in range(1, X):
        got_ref = got_refs[step - 1]
        blocks_ref[step * ROWS : (step + 1) * ROWS] = got_ref[:, :D]
        row_ref[(x_at + X - step) % X] = got_ref[:, D:].astype(F32).T.astype(BF16)


def gather_kernel(parts_ref, out_ref):
    total = parts_ref[0].astype(F32)
    for at in range(1, Z_HI * Y_HI):
        total = total + parts_ref[at].astype(F32)
    total = total.astype(BF16)
    for to in range(Y_HI * Y_LO * Z_LO * CORE):
        out_ref[to] = total


def asking_kernel(weight_ref, own_ref, *refs):
    *states_refs, queries_ref, scores_ref = refs
    states = jnp.concatenate([ref[...] for ref in states_refs], axis=0)
    queries = dot(states, weight_ref[...], (1, 0)).astype(BF16)
    queries_ref[...] = queries
    scores_ref[...] = dot(own_ref[...], queries, (1, 1)) * (D**-0.5)


def part_kernel(place_ref, states_ref, pair_ref, grads_ref, part_ref, stats_ref):
    c_at, y_at = place_ref[1], place_ref[3]
    mine, other = y_at * CORE, (1 - y_at) * CORE
    states, grads = [], []
    for at in range(X):
        states += [states_ref[0, at], states_ref[1, at], pair_ref[0, at], pair_ref[1, at]]
        for source in (mine + c_at, other + c_at, mine + 1 - c_at, other + 1 - c_at):
            grads.append(grads_ref[at * QUARTERS + source, :ROWS])
        stats_ref[at] = grads_ref[at * QUARTERS + mine + c_at, ROWS:, :ROWS]
    states, grads = jnp.concatenate(states, axis=1), jnp.concatenate(grads, axis=0)
    part_ref[...] = dot(states, grads, (1, 0)).astype(BF16)


def passage_kernel(
    place_ref, scores_ref, queries_ref, stats_ref, upper_ref, positive_ref, passage_ref
):
    x_at = place_ref[0]
    row = lax.broadcasted_iota(jnp.int32, (ROWS, ROWS), 0)
    total = jnp.zeros((ROWS, D), F32)
    for stop in range(STOPS):
        x_from = x_at + stop
        here = stats_ref[x_from % X].astype(F32)
        stats = jnp.where(x_from < X, here, upper_ref[x_from % X].astype(F32))
        top = stats[0:1] + stats[1:2] + stats[2:3]
        weight = stats[3:4] + stats[4:5] + stats[5:6]
        cut = slice(stop * ROWS, (stop + 1) * ROWS)
        grad = jnp.exp(scores_ref[:, cut] - top) / weight
        if stop == 0:
            grad = grad - (row == positive_ref[...]).astype(F32)
        total = total + dot(grad.astype(BF16), queries_ref[cut], (1, 0))
    passage_ref[...] = (D**-0.5 * total).astype(BF16)


def finish_kernel(parts_ref, out_ref):
    height = D // MEMBERS // Y_HI
    for y_hi in range(Y_HI):
        for quarter in range(QUARTERS):
            y_lo, c_of = quarter // CORE, quarter % CORE
            total = None
            for z_lo in range(Z_LO):
                block = parts_ref[((y_hi * Y_LO + y_lo) * Z_LO + z_lo) * CORE + c_of].astype(F32)
                total = block if total is None else total + block
            rows = slice(y_hi * height, (y_hi + 1) * height)
            out_ref[rows, quarter * (D // QUARTERS) : (quarter + 1) * (D // QUARTERS)] = total


def around(x, axis, by):
    count = lax.axis_size(axis)
    return lax.ppermute(x, axis, [(i, (i + by) % count) for i in range(count)])


def swap(x, axis):
    return lax.all_to_all(x, axis, split_axis=0, concat_axis=0, tiled=True)


def local(query_states, passages, proj_weight, neg_store, positive, neg_owner, neg_slot, neg_count):
    factor = D**-0.5
    states = query_states.reshape(ROWS, D)
    own = passages.reshape(ROWS, D)
    store = neg_store.reshape(-1, D)
    place = jnp.stack([lax.axis_index(axis) for axis in ("x", "c", "zh", "yl")]).astype(jnp.int32)

    request, used = call(
        plan_kernel,
        (
            jax.ShapeDtypeStruct((MEMBERS, 1, CAP), jnp.int32),
            jax.ShapeDtypeStruct((SLOTS, ROWS), BF16),
        ),
        limit=LARGE,
        moved=1 << 20,
    )(
        neg_owner.reshape(NEG, 1, ROWS),
        neg_slot.reshape(ROWS, NEG).T.reshape(NEG, 1, ROWS),
        neg_count.reshape(1, 1, ROWS),
    )
    mask = used.T
    incoming = swap(request, BLK)

    below = around(own, "zh", 1)
    above = around(states, "zh", -1)
    incoming = lax.optimization_barrier((incoming, below, above))[0]
    served = call(
        serve_kernel,
        jax.ShapeDtypeStruct((MEMBERS, CAP, D), BF16),
        flops=2 * SLOTS * store.shape[0] * D,
        moved=3 << 20,
        limit=LARGE,
        grid=(1,),
        in_specs=[
            pl.BlockSpec((MEMBERS, 1, CAP), lambda i: (0, 0, 0)),
            pl.BlockSpec(store.shape, lambda i: (0, 0)),
        ],
        out_specs=pl.BlockSpec(memory_space=pltpu.HBM),
        scratch_shapes=[
            pltpu.VMEM((PARTS, MEMBERS // PARTS, CAP, D), BF16),
            pltpu.SemaphoreType.DMA((PARTS,)),
        ],
    )(incoming, store)
    replies = swap(served, BLK).reshape(SLOTS, D)

    wide = jax.ShapeDtypeStruct((ROWS, D + D // X), BF16)
    sends = call(
        pack_kernel,
        (wide,) * (X - 1)
        + (jax.ShapeDtypeStruct((ROWS, D), BF16),) * (X - 1)
        + (jax.ShapeDtypeStruct((ROWS, D // X), BF16),),
        scalars=1,
        moved=6 << 20,
    )(place, own, below, above, states)
    mine = sends[-1]
    got = [around(send, "x", step + 1) for step, send in enumerate(sends[: X - 1])]
    blocks, row_states = call(
        unpack_kernel,
        (
            jax.ShapeDtypeStruct((STOPS * ROWS, D), BF16),
            jax.ShapeDtypeStruct((X, D // X, ROWS), BF16),
        ),
        scalars=1,
        moved=4 << 20,
    )(place, own, mine, *got)
    next_states = around(row_states, "yl", 1)
    row_states = jnp.stack([row_states, next_states])
    pair_states = around(row_states, "c", 1)
    late = lax.optimization_barrier((*sends[X - 1 : -1], *got))[: X - 1]
    late = [around(send, "x", step + 1) for step, send in enumerate(late)]
    asking, own_scores = call(
        asking_kernel,
        (
            jax.ShapeDtypeStruct((STOPS * ROWS, D), BF16),
            jax.ShapeDtypeStruct((ROWS, STOPS * ROWS), F32),
        ),
        flops=25 * 10**9,
        moved=4 << 20,
    )(proj_weight, own, states, *late[::-1])
    replies = lax.optimization_barrier((replies, pair_states, own_scores))[0]
    queries = jnp.dot(states, proj_weight, preferred_element_type=F32).astype(BF16)
    scores = dot(queries, blocks, (1, 1)) * factor

    query_grad, quarters = call(
        attend_kernel,
        (
            jax.ShapeDtypeStruct((ROWS, D), BF16),
            jax.ShapeDtypeStruct((X * QUARTERS, ROWS + STAT_ROWS, D // QUARTERS), BF16),
        ),
        limit=LARGE,
        flops=2 * ROWS * D * (2 * SLOTS + STOPS * ROWS),
        moved=4 << 20,
    )(queries, scores, mask, positive.reshape(ROWS, 1), blocks, replies)
    row_grads = swap(quarters, ("x", "yl", "c"))

    part, stats = call(
        part_kernel,
        (
            jax.ShapeDtypeStruct((D // X, D // QUARTERS), BF16),
            jax.ShapeDtypeStruct((X, STAT_ROWS, ROWS), BF16),
        ),
        limit=LARGE,
        scalars=1,
        flops=2 * ROWS * D * D,
        moved=2 << 20,
    )(place, row_states, pair_states, row_grads)
    state_grads = dot(query_grad, proj_weight, (1, 1)).astype(BF16)

    height = D // MEMBERS // Y_HI
    part = swap(part.reshape(Z_HI * Y_HI, height, D // QUARTERS), ("zh", "yh"))
    upper = around(stats, "zh", -1)
    part, state_grads, upper = lax.optimization_barrier((part, state_grads, upper))
    part = call(
        gather_kernel,
        jax.ShapeDtypeStruct((Y_HI * Y_LO * Z_LO * CORE,) + part.shape[1:], BF16),
        limit=LARGE,
        moved=1 << 20,
    )(part)
    upper = lax.optimization_barrier((upper, part))[0]
    passage_grads = call(
        passage_kernel,
        jax.ShapeDtypeStruct((ROWS, D), BF16),
        scalars=1,
        flops=2 * ROWS * D * STOPS * ROWS,
        moved=2 << 20,
    )(place, own_scores, asking, stats, upper, positive.reshape(1, ROWS))

    weight_grad = call(
        finish_kernel,
        jax.ShapeDtypeStruct((D // MEMBERS, D), F32),
        limit=LARGE,
        moved=1 << 20,
    )(swap(part, GRP))
    return (
        state_grads.reshape(query_states.shape),
        passage_grads.reshape(passages.shape),
        weight_grad,
    )


def solution(mesh):
    shape = (Z_HI, X, Y_HI, Y_LO, Z_LO, CORE)
    fine = Mesh(mesh.devices.reshape(shape), ("zh", "x", "yh", "yl", "zl", "c"))
    placed = (
        P(BLK, GRP, None, None),
        P(BLK, GRP, None, None),
        P(),
        P(BLK, GRP, None, None),
        P(BLK, GRP, None),
        P(BLK, GRP, None, None),
        P(BLK, GRP, None, None),
        P(BLK, GRP, None),
    )
    return jax.shard_map(
        local,
        mesh=fine,
        in_specs=placed,
        out_specs=(P(BLK, GRP, None, None), P(BLK, GRP, None, None), P(BLK, None)),
        check_vma=False,
    )
```

```python
import jax
import jax.numpy as jnp
from jax import lax
from jax.experimental import pallas as pl
from jax.experimental.pallas import tpu as pltpu
from jax.sharding import Mesh, PartitionSpec as P

STOPS = 4
NEG = 7
CAP = 64
ROWS = 128
D = 1024
Z_HI, X, Y_HI, Y_LO, Z_LO, CORE = 4, 4, 4, 2, 3, 2
QUARTERS = Y_LO * CORE
MEMBERS = Z_HI * X
SLOTS = MEMBERS * CAP
BLK = ("zh", "x")
GRP = ("yh", "yl", "zl", "c")
F32 = jnp.float32
BF16 = jnp.bfloat16
LARGE = 58
STAT_ROWS = 16
PARTS = 4


def whole(x):
    return pl.BlockSpec(x.shape, lambda i, rank=len(x.shape): (0,) * rank)


def call(kernel, out_shape, *, scalars=0, flops=0, moved=0, limit=16, **kwargs):
    def run(*args):
        if "grid" not in kwargs:
            specs = [pl.BlockSpec(memory_space=pltpu.SMEM)] * scalars
            specs += [whole(arg) for arg in args[scalars:]]
            outs = jax.tree.map(whole, out_shape)
            spec = {"grid": (1,), "in_specs": specs, "out_specs": outs} | kwargs
        else:
            spec = kwargs
        return pl.pallas_call(
            kernel,
            out_shape=out_shape,
            compiler_params=pltpu.CompilerParams(vmem_limit_bytes=limit * 1024 * 1024),
            cost_estimate=pl.CostEstimate(flops=flops, bytes_accessed=moved, transcendentals=0),
            **spec,
        )(*args)

    return run


def dot(left, right, on):
    return lax.dot_general(left, right, ((on[:1], on[1:]), ((), ())), preferred_element_type=F32)


def plan_kernel(owner_ref, slot_ref, count_ref, request_ref, used_ref):
    lanes = ROWS
    row8 = lax.broadcasted_iota(jnp.int32, (8, lanes), 0)
    lane8 = lax.broadcasted_iota(jnp.int32, (8, lanes), 1)
    row = lax.broadcasted_iota(jnp.int32, (lanes, lanes), 0)
    lane = lax.broadcasted_iota(jnp.int32, (lanes, lanes), 1)

    def bits(value):
        return value.astype(F32).astype(BF16)

    owner = jnp.zeros((8, lanes), F32)
    for at in range(NEG):
        flat = owner_ref[at]
        kept = jnp.where((lane8 + at * lanes) % NEG == row8, flat, 0)
        owner = owner + dot(bits(kept), bits((row + at * lanes) // NEG == lane), (1, 0))
    owner = jnp.where(row8 < NEG, owner.astype(jnp.int32), -1)
    named = (jnp.concatenate([owner] * MEMBERS, axis=0) == row // 8).astype(F32)
    before = dot(bits(named), bits(row < lane), (1, 0))
    above = bits((row // 8 == lane // 8) & (row > lane))
    base = jnp.sum(dot(above, bits(named), (1, 0)), axis=1, keepdims=True)
    place = named * (before + base + (row // 8 * CAP).astype(F32))
    placed = place[:8]
    for at in range(1, MEMBERS):
        placed = placed + place[at * 8 : (at + 1) * 8]
    placed = placed.astype(jnp.int32)
    live = (row8 < count_ref[0]).astype(F32)
    column = lax.broadcasted_iota(jnp.int32, (SLOTS, lanes), 0)
    wanted = jnp.zeros((SLOTS, lanes), jnp.int32)
    used = jnp.zeros((SLOTS, lanes), F32)
    for j in range(NEG):
        match = column == placed[j : j + 1]
        wanted = wanted + jnp.where(match, slot_ref[j], 0)
        used = used + jnp.where(match, live[j : j + 1], 0.0)
    used_ref[...] = used.astype(BF16)
    ones = jnp.ones((8, lanes), BF16)
    high = dot(ones, bits(wanted // 256), (1, 1))[:1]
    low = dot(ones, bits(wanted % 256), (1, 1))[:1]
    request = (high * 256.0 + low).astype(jnp.int32)
    for owner_at in range(MEMBERS):
        request_ref[owner_at] = request[:, owner_at * CAP : (owner_at + 1) * CAP]


def serve_kernel(incoming_ref, store_ref, served_hbm, rows_ref, sems):
    pool = store_ref.shape[0]
    group = MEMBERS // PARTS
    row = lax.broadcasted_iota(jnp.int32, (pool, group * CAP), 0)
    sends = []
    for at in range(PARTS):
        wanted = [incoming_ref[at * group + k] for k in range(group)]
        pick = (row == jnp.concatenate(wanted, axis=1)).astype(F32).astype(BF16)
        rows = dot(pick, store_ref[...], (0, 0)).astype(BF16)
        rows_ref[at] = rows.reshape(group, CAP, D)
        target = served_hbm.at[pl.ds(at * group, group)]
        sends.append(pltpu.make_async_copy(rows_ref.at[at], target, sems.at[at]))
        sends[-1].start()
    for send in sends:
        send.wait()


def in_three(value):
    first = value.astype(BF16).astype(F32)
    second = (value - first).astype(BF16).astype(F32)
    return first, second, value - first - second


def attend_kernel(
    queries_ref, scores_ref, mask_ref, positive_ref, blocks_ref, replies_ref, query_ref, quarters_ref
):
    factor = D**-0.5
    batch_scores = scores_ref[...]
    neg_scores = dot(queries_ref[...], replies_ref[...], (1, 1)) * factor
    neg_scores = jnp.where(mask_ref[...].astype(F32) > 0.5, neg_scores, -jnp.inf)
    top = jnp.maximum(
        jnp.max(batch_scores, axis=1, keepdims=True), jnp.max(neg_scores, axis=1, keepdims=True)
    )
    batch_exp = jnp.exp(batch_scores - top)
    neg_exp = jnp.exp(neg_scores - top)
    total = jnp.sum(batch_exp, axis=1, keepdims=True) + jnp.sum(neg_exp, axis=1, keepdims=True)
    column = lax.broadcasted_iota(jnp.int32, (ROWS, STOPS * ROWS), 1)
    hit = (column == positive_ref[...]).astype(F32)
    batch_grad = (batch_exp / total - hit).astype(BF16)
    neg_grad = (neg_exp / total).astype(BF16)
    inner = dot(batch_grad, blocks_ref[...], (1, 0)) + dot(neg_grad, replies_ref[...], (1, 0))
    query_grad = (factor * inner).astype(BF16)
    query_ref[...] = query_grad

    lane = lax.broadcasted_iota(jnp.int32, (ROWS, ROWS), 1)
    row = lax.broadcasted_iota(jnp.int32, (ROWS, ROWS), 0)
    stats = jnp.zeros((ROWS, ROWS), F32)
    for at, value in enumerate(in_three(top) + in_three(total)):
        stats = jnp.where(lane == at, value, stats)
    turned = dot(stats.astype(BF16), (lane == row).astype(F32).astype(BF16), (0, 0))
    turned = turned[:STAT_ROWS].astype(BF16)
    rest = jnp.zeros((STAT_ROWS, D // QUARTERS - ROWS), BF16)
    turned = jnp.concatenate([turned, rest], axis=1)
    for to in range(X * QUARTERS):
        at = to % QUARTERS * (D // QUARTERS)
        quarters_ref[to, :ROWS] = query_grad[:, at : at + D // QUARTERS]
        quarters_ref[to, ROWS:] = turned


def pack_kernel(place_ref, own_ref, below_ref, states_ref, *refs):
    x_at = place_ref[0]
    share = D // MEMBERS

    def columns(x_to):
        piece = None
        for x_of in range(X):
            cut = [states_ref[:, (z * X + x_of) * share :][:, :share] for z in range(Z_HI)]
            cut = jnp.concatenate(cut, axis=1)
            piece = cut if piece is None else jnp.where(x_to == x_of, cut, piece)
        return piece

    *first_refs, mine_ref = refs
    mine_ref[...] = columns(x_at)
    for step in range(1, X):
        first_ref = first_refs[step - 1]
        first_ref[:, :D] = jnp.where(x_at + step >= X, below_ref[...], own_ref[...])
        first_ref[:, D:] = columns((x_at + step) % X)


def second_kernel(place_ref, above_ref, states_ref, *refs):
    for step in range(1, X):
        wraps = place_ref[0] + step >= X
        refs[step - 1][...] = jnp.where(wraps, states_ref[...], above_ref[...])


def unpack_kernel(place_ref, own_ref, mine_ref, *refs):
    *got_refs, blocks_ref, row_ref = refs
    x_at = place_ref[0]
    blocks_ref[:ROWS] = own_ref[...]
    row_ref[x_at] = mine_ref[...].astype(F32).T.astype(BF16)
    for step in range(1, X):
        got_ref = got_refs[step - 1]
        blocks_ref[step * ROWS : (step + 1) * ROWS] = got_ref[:, :D]
        row_ref[(x_at + X - step) % X] = got_ref[:, D:].astype(F32).T.astype(BF16)


def gather_kernel(parts_ref, out_ref):
    total = parts_ref[0].astype(F32)
    for at in range(1, Z_HI * Y_HI):
        total = total + parts_ref[at].astype(F32)
    total = total.astype(BF16)
    for to in range(Y_HI * Y_LO * Z_LO * CORE):
        out_ref[to] = total


def asking_kernel(weight_ref, own_ref, *refs):
    *states_refs, queries_ref, scores_ref = refs
    states = jnp.concatenate([ref[...] for ref in states_refs], axis=0)
    queries = dot(states, weight_ref[...], (1, 0)).astype(BF16)
    queries_ref[...] = queries
    scores_ref[...] = dot(own_ref[...], queries, (1, 1)) * (D**-0.5)


def part_kernel(place_ref, states_ref, pair_ref, grads_ref, part_ref, stats_ref):
    c_at, y_at = place_ref[1], place_ref[3]
    mine, other = y_at * CORE, (1 - y_at) * CORE
    states, grads = [], []
    for at in range(X):
        states += [states_ref[0, at], states_ref[1, at], pair_ref[0, at], pair_ref[1, at]]
        for source in (mine + c_at, other + c_at, mine + 1 - c_at, other + 1 - c_at):
            grads.append(grads_ref[at * QUARTERS + source, :ROWS])
        stats_ref[at] = grads_ref[at * QUARTERS + mine + c_at, ROWS:, :ROWS]
    states, grads = jnp.concatenate(states, axis=1), jnp.concatenate(grads, axis=0)
    part_ref[...] = dot(states, grads, (1, 0)).astype(BF16)


def passage_kernel(
    place_ref, scores_ref, queries_ref, stats_ref, upper_ref, positive_ref, passage_ref
):
    x_at = place_ref[0]
    row = lax.broadcasted_iota(jnp.int32, (ROWS, ROWS), 0)
    total = jnp.zeros((ROWS, D), F32)
    for stop in range(STOPS):
        x_from = x_at + stop
        here = stats_ref[x_from % X].astype(F32)
        stats = jnp.where(x_from < X, here, upper_ref[x_from % X].astype(F32))
        top = stats[0:1] + stats[1:2] + stats[2:3]
        weight = stats[3:4] + stats[4:5] + stats[5:6]
        cut = slice(stop * ROWS, (stop + 1) * ROWS)
        grad = jnp.exp(scores_ref[:, cut] - top) / weight
        if stop == 0:
            grad = grad - (row == positive_ref[...]).astype(F32)
        total = total + dot(grad.astype(BF16), queries_ref[cut], (1, 0))
    passage_ref[...] = (D**-0.5 * total).astype(BF16)


def finish_kernel(parts_ref, out_ref):
    height = D // MEMBERS // Y_HI
    for y_hi in range(Y_HI):
        for quarter in range(QUARTERS):
            y_lo, c_of = quarter // CORE, quarter % CORE
            total = None
            for z_lo in range(Z_LO):
                block = parts_ref[((y_hi * Y_LO + y_lo) * Z_LO + z_lo) * CORE + c_of].astype(F32)
                total = block if total is None else total + block
            rows = slice(y_hi * height, (y_hi + 1) * height)
            out_ref[rows, quarter * (D // QUARTERS) : (quarter + 1) * (D // QUARTERS)] = total


def around(x, axis, by):
    count = lax.axis_size(axis)
    return lax.ppermute(x, axis, [(i, (i + by) % count) for i in range(count)])


def swap(x, axis):
    return lax.all_to_all(x, axis, split_axis=0, concat_axis=0, tiled=True)


def local(query_states, passages, proj_weight, neg_store, positive, neg_owner, neg_slot, neg_count):
    factor = D**-0.5
    states = query_states.reshape(ROWS, D)
    own = passages.reshape(ROWS, D)
    store = neg_store.reshape(-1, D)
    place = jnp.stack([lax.axis_index(axis) for axis in ("x", "c", "zh", "yl")]).astype(jnp.int32)

    request, used = call(
        plan_kernel,
        (
            jax.ShapeDtypeStruct((MEMBERS, 1, CAP), jnp.int32),
            jax.ShapeDtypeStruct((SLOTS, ROWS), BF16),
        ),
        limit=LARGE,
        moved=1 << 20,
    )(
        neg_owner.reshape(NEG, 1, ROWS),
        neg_slot.reshape(ROWS, NEG).T.reshape(NEG, 1, ROWS),
        neg_count.reshape(1, 1, ROWS),
    )
    mask = used.T
    incoming = swap(request, BLK)

    below = around(own, "zh", 1)
    incoming = lax.optimization_barrier((incoming, below))[0]
    above = around(lax.optimization_barrier((states, incoming))[0], "zh", -1)
    served = call(
        serve_kernel,
        jax.ShapeDtypeStruct((MEMBERS, CAP, D), BF16),
        flops=2 * SLOTS * store.shape[0] * D,
        moved=3 << 20,
        limit=LARGE,
        grid=(1,),
        in_specs=[
            pl.BlockSpec((MEMBERS, 1, CAP), lambda i: (0, 0, 0)),
            pl.BlockSpec(store.shape, lambda i: (0, 0)),
        ],
        out_specs=pl.BlockSpec(memory_space=pltpu.HBM),
        scratch_shapes=[
            pltpu.VMEM((PARTS, MEMBERS // PARTS, CAP, D), BF16),
            pltpu.SemaphoreType.DMA((PARTS,)),
        ],
    )(incoming, store)
    replies = swap(served, BLK).reshape(SLOTS, D)

    wide = jax.ShapeDtypeStruct((ROWS, D + D // X), BF16)
    sends = call(
        pack_kernel,
        (wide,) * (X - 1) + (jax.ShapeDtypeStruct((ROWS, D // X), BF16),),
        scalars=1,
        moved=4 << 20,
    )(place, own, lax.optimization_barrier((below, served))[0], states)
    mine = sends[-1]
    second = call(
        second_kernel,
        (jax.ShapeDtypeStruct((ROWS, D), BF16),) * (X - 1),
        scalars=1,
        flops=32 * 10**9,
        moved=4 << 20,
    )(place, above, states)
    got = [around(send, "x", step + 1) for step, send in enumerate(sends[: X - 1])]
    blocks, row_states = call(
        unpack_kernel,
        (
            jax.ShapeDtypeStruct((STOPS * ROWS, D), BF16),
            jax.ShapeDtypeStruct((X, D // X, ROWS), BF16),
        ),
        scalars=1,
        moved=4 << 20,
    )(place, own, mine, *got)
    next_states = around(row_states, "yl", 1)
    row_states = jnp.stack([row_states, next_states])
    pair_states = around(row_states, "c", 1)
    late = lax.optimization_barrier((*second, *got))[: X - 1]
    late = [around(send, "x", step + 1) for step, send in enumerate(late)]
    asking, own_scores = call(
        asking_kernel,
        (
            jax.ShapeDtypeStruct((STOPS * ROWS, D), BF16),
            jax.ShapeDtypeStruct((ROWS, STOPS * ROWS), F32),
        ),
        flops=25 * 10**9,
        moved=4 << 20,
    )(proj_weight, own, states, *late[::-1])
    replies = lax.optimization_barrier((replies, pair_states, own_scores))[0]
    queries = jnp.dot(states, proj_weight, preferred_element_type=F32).astype(BF16)
    scores = dot(queries, blocks, (1, 1)) * factor

    query_grad, quarters = call(
        attend_kernel,
        (
            jax.ShapeDtypeStruct((ROWS, D), BF16),
            jax.ShapeDtypeStruct((X * QUARTERS, ROWS + STAT_ROWS, D // QUARTERS), BF16),
        ),
        limit=LARGE,
        flops=2 * ROWS * D * (2 * SLOTS + STOPS * ROWS),
        moved=4 << 20,
    )(queries, scores, mask, positive.reshape(ROWS, 1), blocks, replies)
    row_grads = swap(quarters, ("x", "yl", "c"))

    part, stats = call(
        part_kernel,
        (
            jax.ShapeDtypeStruct((D // X, D // QUARTERS), BF16),
            jax.ShapeDtypeStruct((X, STAT_ROWS, ROWS), BF16),
        ),
        limit=LARGE,
        scalars=1,
        flops=2 * ROWS * D * D,
        moved=2 << 20,
    )(place, row_states, pair_states, row_grads)
    state_grads = dot(query_grad, proj_weight, (1, 1)).astype(BF16)

    height = D // MEMBERS // Y_HI
    part = swap(part.reshape(Z_HI * Y_HI, height, D // QUARTERS), ("zh", "yh"))
    upper = around(stats, "zh", -1)
    part, state_grads, upper = lax.optimization_barrier((part, state_grads, upper))
    part = call(
        gather_kernel,
        jax.ShapeDtypeStruct((Y_HI * Y_LO * Z_LO * CORE,) + part.shape[1:], BF16),
        limit=LARGE,
        moved=1 << 20,
    )(part)
    upper = lax.optimization_barrier((upper, part))[0]
    passage_grads = call(
        passage_kernel,
        jax.ShapeDtypeStruct((ROWS, D), BF16),
        scalars=1,
        flops=2 * ROWS * D * STOPS * ROWS,
        moved=2 << 20,
    )(place, own_scores, asking, stats, upper, positive.reshape(1, ROWS))

    weight_grad = call(
        finish_kernel,
        jax.ShapeDtypeStruct((D // MEMBERS, D), F32),
        limit=LARGE,
        moved=1 << 20,
    )(swap(part, GRP))
    return (
        state_grads.reshape(query_states.shape),
        passage_grads.reshape(passages.shape),
        weight_grad,
    )


def solution(mesh):
    shape = (Z_HI, X, Y_HI, Y_LO, Z_LO, CORE)
    fine = Mesh(mesh.devices.reshape(shape), ("zh", "x", "yh", "yl", "zl", "c"))
    placed = (
        P(BLK, GRP, None, None),
        P(BLK, GRP, None, None),
        P(),
        P(BLK, GRP, None, None),
        P(BLK, GRP, None),
        P(BLK, GRP, None, None),
        P(BLK, GRP, None, None),
        P(BLK, GRP, None),
    )
    return jax.shard_map(
        local,
        mesh=fine,
        in_specs=placed,
        out_specs=(P(BLK, GRP, None, None), P(BLK, GRP, None, None), P(BLK, None)),
        check_vma=False,
    )
```
